256 devices in a mesh: tm: 32 (over y, x, core), space: 8 (over z).
Axes of the slice: x: 4, y: 4, z: 8, core: 2. Of those that a mesh axis runs over, the one named last changes fastest.
Arguments:
- initial_state: float32 [256, 2048], P('space'), may hold values from -6 to 6
- guesses: float32 [32, 256, 2048], P('tm', 'space'), may hold values from -6 to 6
- diffusivity: float32 [256, 2048], P('space'), may hold values from 0.0125 to 0.025
- forcing_field: float32 [256, 2048], P('space'), may hold values from -1 to 1
- amplitudes: float32 [256], P('tm'), may hold values from 0.5 to 1.5
Outputs:
- corrected: float32 [32, 256, 2048], P('tm', 'space')
The draws below stay inside these ranges and needn't reach their ends.
All inputs are finite; a program needn't handle non-finite values.
Results may differ from the reference program's by a relative error of at most 0.00002.
Values sent between devices are 32-bit elements; how exact they have to be, the bound alone decides.
A program may use at most 64 MiB of HBM per device.

```python
import math
import jax
import jax.numpy as jnp
from jax import lax

COLS = 2048
STEPS = 8
SLABS = 32
NR = 256
NT = 256
N_TM = 32


def block_levels(rng, dims, split, least, top_value):
    loudness, own = 1.0, jax.random.fold_in(rng, 6)
    for dim, blocks in split:
        heights = jnp.exp(jax.random.uniform(jax.random.fold_in(own, dim), (blocks,), jnp.float32, least / len(split), top_value / len(split)))
        loudness = loudness * jnp.repeat(heights, dims[dim] // blocks).reshape([-1 if axis == dim else 1 for axis in range(len(dims))])
    return loudness


def scatter_about(stream_key, dims, width, reach, cuts=(), kind=jnp.bfloat16):
    entries = jax.random.normal(stream_key, dims, jnp.float32) * width
    if len(cuts) > 0:
        entries = block_levels(stream_key, dims, cuts, -0.22, 0.18) * entries
    return jnp.clip(entries, min=-reach, max=reach).astype(kind)


def setup_inputs(seed: int = 0) -> dict:
    seeds = jax.random.split(jax.random.key(seed), 6)
    initial_state = scatter_about(seeds[0], (NR, COLS), 1.0, 6.0, ((0, 8),), jnp.float32)
    guesses = scatter_about(seeds[1], (SLABS, NR, COLS), 1.0, 6.0, ((0, 32), (1, 8)), jnp.float32)
    diffusivity = jnp.clip(jnp.exp(math.log(0.025) - 0.6931472 * jax.random.uniform(seeds[2], (NR, COLS), jnp.float32) ** block_levels(seeds[2], (NR, COLS), ((0, 8),), -0.2, 0.2)), 0.0125, 0.025)
    forcing_field = scatter_about(seeds[3], (NR, COLS), 0.125, 1.0, ((0, 8),), jnp.float32)
    amplitudes = jnp.clip(0.5 + 1.0 * jax.random.uniform(seeds[4], (NT,), jnp.float32) ** block_levels(seeds[4], (NT,), ((0, 32),), -0.2, 0.2), 0.5, 1.5)
    return {"initial_state": initial_state, "guesses": guesses, "diffusivity": diffusivity, "forcing_field": forcing_field, "amplitudes": amplitudes}


ADVECT = 0.01


def advance(padded, diffusivity, factor, forcing):
    center = padded[..., 1:-1, :]
    above_rows = padded[..., :-2, :]
    below_rows = padded[..., 2:, :]
    left_cols = jnp.roll(center, 1, axis=-1)
    right_cols = jnp.roll(center, -1, axis=-1)
    laplace_term = above_rows + below_rows + left_cols + right_cols - 4.0 * center
    return (center + factor * diffusivity * laplace_term
            - factor * ADVECT * (center - above_rows)
            - factor * ADVECT * (center - left_cols) + forcing)


def reference(initial_state, guesses, diffusivity, forcing_field, amplitudes):
    plan = amplitudes.reshape(N_TM, STEPS)
    current = jnp.concatenate([initial_state[None], guesses[:-1]], axis=0)
    for k in range(STEPS):
        padded = jnp.pad(current, ((0, 0), (1, 1), (0, 0)))
        current = advance(padded, diffusivity, 1.0, plan[:, k][:, None, None] * forcing_field)
    residual = current - guesses

    def coarse_turn(error_field, residual_now):
        padded_error = jnp.pad(error_field, ((1, 1), (0, 0)))
        update = advance(padded_error, diffusivity, float(STEPS), 0.0) + residual_now
        return update, update

    start_error = jnp.zeros(guesses.shape[1:], jnp.float32)
    _, correction = lax.scan(coarse_turn, start_error, residual)
    return guesses + correction
```

```python
import functools

import jax
import jax.numpy as jnp
from jax import lax
from jax.experimental import pallas as pl
from jax.experimental.pallas import tpu as pltpu
from jax.sharding import PartitionSpec as P

MESH = pl.DeviceIdType.MESH
ADVECT = 0.01
LANES = 128
STEPS = 8
SPAN = 8
ROWS = 32
HALO = STEPS + SPAN
TALL = ROWS + 2 * HALO
TRIM = TALL - 2 * STEPS
SIDE = 32
OWN = LANES - 2 * SIDE


def shifted(u):
    rows = u.shape[0]
    up_left = pltpu.roll(u, 1, 0) + pltpu.roll(u, 1, 1)
    down_right = pltpu.roll(u, rows - 1, 0) + pltpu.roll(u, LANES - 1, 1)
    return up_left, down_right


def lanes_of(shape):
    return lax.broadcasted_iota(jnp.int32, shape, 1)


def kernel(
    nt, nz, initial_hbm, guess_hbm, kappa_hbm, forcing_hbm, amp_ref, out_ref,
    guess, pairs, windows, params, states, coarse, fine, amps, residual, error, edges, packed, arrived,
    load_sem, pair_sem, win_send, win_recv, par_send, par_recv, z_send, z_recv, edge_send, edge_recv, back_send, back_recv,
):
    tm, z = lax.axis_index("tm"), lax.axis_index("space")
    tiles = guess.shape[1] // LANES
    has_up, has_down = z > 0, z < nz - 1
    before, after = lax.rem(tm + nt - 1, nt), lax.rem(tm + 1, nt)

    barrier = pltpu.get_barrier_semaphore()

    def greet(t, where):
        pl.semaphore_signal(barrier, inc=1, device_id=(t, where), device_id_type=MESH)

    def greet_plane(k, carry):
        greet(lax.rem(tm + k, nt), z)
        return carry

    lax.fori_loop(1, nt, greet_plane, 0)

    @pl.when(has_up)
    def _():
        for t in (tm, before, after):
            greet(t, z - 1)

    @pl.when(has_down)
    def _():
        for t in (tm, before, after):
            greet(t, z + 1)

    load_guess = pltpu.make_async_copy(guess_hbm.at[0], guess, load_sem)
    load_guess.start()
    first = lax.rem(lax.div(tm + nt - 1, 2), tiles)
    second = lax.rem(first + 1, tiles)
    loads = []
    for i, ref in enumerate((initial_hbm, kappa_hbm, forcing_hbm)):
        for k, tile in enumerate((first, second)):
            columns = pl.ds(pl.multiple_of(tile * LANES, LANES), LANES)
            loads.append(pltpu.make_async_copy(ref.at[:, columns], pairs.at[i, k], pair_sem.at[i, k]))
    for load in loads:
        load.start()

    @pl.when(jnp.logical_not(has_up))
    def _():
        params[:, :HALO, :] = jnp.zeros((3, HALO, LANES), jnp.float32)
        states[:, :HALO, :] = jnp.zeros((nt + 1, HALO, LANES), jnp.float32)

    @pl.when(jnp.logical_not(has_down))
    def _():
        params[:, HALO + ROWS :, :] = jnp.zeros((3, HALO, LANES), jnp.float32)
        states[:, HALO + ROWS :, :] = jnp.zeros((nt + 1, HALO, LANES), jnp.float32)

    row_index = lax.broadcasted_iota(jnp.int32, (ROWS, LANES), 0)
    lane = lanes_of((ROWS, LANES))
    marks = jnp.zeros((ROWS, LANES), jnp.float32)
    for k in range(STEPS):
        marks = jnp.where(row_index == k, amp_ref[k], marks)
    marked = (lane == 0) & (row_index < STEPS)

    load_guess.wait()

    def tile_of(i):
        return guess[:, pl.ds(pl.multiple_of(i * LANES, LANES), LANES)]

    def cut(i, carry):
        low, mid, high = (tile_of(lax.rem(i + d, tiles)) for d in (tiles - 1, 0, 1))
        even = jnp.where(lane < SIDE, pltpu.roll(low, SIDE, 1), pltpu.roll(mid, SIDE, 1))
        odd = jnp.where(lane < LANES - SIDE, pltpu.roll(mid, LANES - SIDE, 1), pltpu.roll(high, LANES - SIDE, 1))
        windows[2 * i] = jnp.where(marked, marks, even)
        windows[2 * i + 1] = jnp.where(marked, marks, odd)
        return carry

    lax.fori_loop(0, tiles, cut, 0)
    pl.semaphore_wait(barrier, nt - 1 + 3 * has_up.astype(jnp.int32) + 3 * has_down.astype(jnp.int32))

    body = pl.ds(HALO, ROWS)

    def window_copy(source, target):
        return pltpu.make_async_remote_copy(
            windows.at[target], states.at[source + 1, body], win_send.at[target], win_recv.at[source],
            device_id=(target, z), device_id_type=MESH,
        )

    def send_window(k, carry):
        window_copy(tm, lax.rem(tm + k, nt)).start()
        return carry

    lax.fori_loop(1, nt, send_window, 0)
    states[tm + 1, HALO : HALO + ROWS, :] = windows[tm]

    for load in loads:
        load.wait()
    shift = jnp.where(lax.rem(tm, 2) == 0, SIDE, LANES - SIDE)
    for i in range(3):
        low, high = pltpu.roll(pairs[i, 0], shift, 1), pltpu.roll(pairs[i, 1], shift, 1)
        value = jnp.where(lane < shift, low, high)
        if i == 0:
            states[0, HALO : HALO + ROWS, :] = value
        params[i, HALO : HALO + ROWS, :] = value

    def params_up():
        return pltpu.make_async_remote_copy(
            params.at[:, pl.ds(HALO, HALO)], params.at[:, pl.ds(HALO + ROWS, HALO)], par_send.at[0], par_recv.at[0],
            device_id=(tm, z - 1), device_id_type=MESH,
        )

    def params_down():
        return pltpu.make_async_remote_copy(
            params.at[:, pl.ds(ROWS, HALO)], params.at[:, pl.ds(0, HALO)], par_send.at[1], par_recv.at[1],
            device_id=(tm, z + 1), device_id_type=MESH,
        )

    def state_up(t):
        return pltpu.make_async_remote_copy(
            states.at[t, pl.ds(HALO, HALO)], states.at[t, pl.ds(HALO + ROWS, HALO)], z_send.at[0, t], z_recv.at[0, t],
            device_id=(tm, z - 1), device_id_type=MESH,
        )

    def state_down(t):
        return pltpu.make_async_remote_copy(
            states.at[t, pl.ds(ROWS, HALO)], states.at[t, pl.ds(0, HALO)], z_send.at[1, t], z_recv.at[1, t],
            device_id=(tm, z + 1), device_id_type=MESH,
        )

    @pl.when(has_up)
    def _():
        params_up().start()

    @pl.when(has_down)
    def _():
        params_down().start()

    def forward(t, carry):
        @pl.when(t != tm)
        def _():
            window_copy(t, tm).wait_recv()

        @pl.when(has_up)
        def _():
            state_up(t + 1).start()

        @pl.when(has_down)
        def _():
            state_down(t + 1).start()

        return carry

    lax.fori_loop(0, nt, forward, 0)

    @pl.when(has_down)
    def _():
        params_up().wait_recv()

    @pl.when(has_up)
    def _():
        params_down().wait_recv()

    states[0, :HALO, :] = params[0, :HALO, :]
    states[0, HALO + ROWS :, :] = params[0, HALO + ROWS :, :]
    rows = lax.broadcasted_iota(jnp.int32, (TALL, LANES), 0)
    inside = ((rows >= HALO) | has_up) & ((rows < HALO + ROWS) | has_down)
    kappa = params[1]
    for ref, factor in ((fine, 1.0), (coarse, float(STEPS))):
        trim = slice(0, TALL) if ref is fine else slice(STEPS, STEPS + TRIM)
        ref[0] = jnp.where(inside, 1.0 - factor * (4.0 * kappa + 2.0 * ADVECT), 0.0)[trim]
        ref[1] = jnp.where(inside, factor * (kappa + ADVECT), 0.0)[trim]
        ref[2] = jnp.where(inside, factor * kappa, 0.0)[trim]
    fine[3] = jnp.where(inside, params[2], 0.0)

    def relax(t, carry):
        @pl.when(has_down)
        def _():
            state_up(t + 1).wait_recv()

        @pl.when(has_up)
        def _():
            state_down(t + 1).wait_recv()

        amps[...] = jnp.broadcast_to(states[t + 1, HALO : HALO + STEPS, 0:1], (STEPS, LANES))
        u = states[t]
        for k in range(STEPS):
            up_left, down_right = shifted(u)
            u = fine[0] * u + fine[1] * up_left + fine[2] * down_right + amps[k : k + 1, :] * fine[3]
        residual[t] = u[STEPS : STEPS + TRIM] - states[t + 1, STEPS : STEPS + TRIM, :]
        return carry

    def back_copy(source, target):
        return pltpu.make_async_remote_copy(
            packed.at[target], arrived.at[source], back_send.at[target], back_recv.at[source],
            device_id=(target, z), device_id_type=MESH,
        )

    half = ROWS // 2
    lane_half = lanes_of((half, LANES))

    def sweep(t, e):
        up_left, down_right = shifted(e)
        e = coarse[0] * e + coarse[1] * up_left + coarse[2] * down_right + residual[t]
        top, bottom = e[SPAN : SPAN + half], e[SPAN + half : SPAN + ROWS]
        both = jnp.where(lane_half < OWN, pltpu.roll(top, LANES - SIDE, 1), pltpu.roll(bottom, SIDE, 1))

        @pl.when(t == tm)
        def _():
            arrived[t] = both

        @pl.when(t != tm)
        def _():
            packed[t] = both
            back_copy(tm, t).start()

        return e

    edge_rows = {-1: (pl.ds(SPAN, SPAN), pl.ds(SPAN + ROWS, SPAN)), 1: (pl.ds(ROWS, SPAN), pl.ds(0, SPAN)), 0: (pl.ds(SPAN, ROWS), pl.ds(SPAN, ROWS))}

    def edge_copies(s):
        for dz in (-1, 0, 1):
            for slot, target in ((2, before), (1, tm), (0, after)):
                if dz == 0 and slot == 1:
                    continue
                here, there = edge_rows[dz]
                copy = pltpu.make_async_remote_copy(
                    error.at[s, here], edges.at[s, slot, there], edge_send.at[s, slot, dz + 1], edge_recv.at[s, slot, dz + 1],
                    device_id=(target, z + dz), device_id_type=MESH,
                )
                yield dz, copy

    def when_dz(dz, send, do):
        if dz == 0:
            do()
        else:
            up = (dz == -1) == send
            pl.when(has_up if up else has_down)(do)

    stages = nt // SPAN
    lane_trim = lanes_of((TRIM, LANES))
    row_trim = lax.broadcasted_iota(jnp.int32, (TRIM, LANES), 0)
    centre = (row_trim >= SPAN) & (row_trim < SPAN + ROWS)

    e = jnp.zeros((TRIM, LANES), jnp.float32)
    for s in range(stages):
        lax.fori_loop(s * SPAN, (s + 1) * SPAN, relax, 0)
        if s > 0:
            for dz, copy in edge_copies(s - 1):
                when_dz(dz, False, copy.wait_recv)
            left = pltpu.roll(edges[s - 1, 0], OWN, 1)
            right = pltpu.roll(edges[s - 1, 2], OWN, 1)
            own = jnp.where(centre, error[s - 1], edges[s - 1, 1])
            e = jnp.where(lane_trim < SIDE, left, jnp.where(lane_trim >= LANES - SIDE, right, own))
        e = lax.fori_loop(s * SPAN, (s + 1) * SPAN, sweep, e)
        if s < stages - 1:
            error[s] = e
            for slot in range(3):
                @pl.when(jnp.logical_not(has_up))
                def _():
                    edges[s, slot, :SPAN, :] = jnp.zeros((SPAN, LANES), jnp.float32)

                @pl.when(jnp.logical_not(has_down))
                def _():
                    edges[s, slot, SPAN + ROWS :, :] = jnp.zeros((SPAN, LANES), jnp.float32)

            for dz, copy in edge_copies(s):
                when_dz(dz, True, copy.start)

    def collect(k, carry):
        back_copy(lax.rem(tm + k, nt), tm).wait_recv()
        return carry

    lax.fori_loop(1, nt, collect, 0)

    def join(i, carry):
        first, second = arrived[2 * i], arrived[2 * i + 1]
        columns = pl.ds(pl.multiple_of(i * LANES, LANES), LANES)
        top = jnp.where(lane_half < OWN, first, pltpu.roll(second, OWN, 1))
        bottom = jnp.where(lane_half < OWN, pltpu.roll(first, OWN, 1), second)
        out_ref[0, :half, columns] = guess[:half, columns] + top
        out_ref[0, half:, columns] = guess[half:, columns] + bottom
        return carry

    lax.fori_loop(0, tiles, join, 0)

    def sent(k, carry):
        t = lax.rem(tm + k, nt)
        window_copy(tm, t).wait_send()
        back_copy(tm, t).wait_send()
        return carry

    lax.fori_loop(1, nt, sent, 0)

    @pl.when(has_up)
    def _():
        params_up().wait_send()
        lax.fori_loop(1, nt + 1, lambda t, carry: (state_up(t).wait_send(), carry)[1], 0)

    @pl.when(has_down)
    def _():
        params_down().wait_send()
        lax.fori_loop(1, nt + 1, lambda t, carry: (state_down(t).wait_send(), carry)[1], 0)

    for s in range(stages - 1):
        for dz, copy in edge_copies(s):
            when_dz(dz, True, copy.wait_send)


def per_device(initial_state, guesses, diffusivity, forcing_field, amplitudes):
    nt, nz = lax.axis_size("tm"), lax.axis_size("space")
    rows, cols = initial_state.shape
    stages = nt // SPAN
    dma = pltpu.SemaphoreType.DMA
    vmem = functools.partial(pltpu.VMEM, dtype=jnp.float32)
    hbm = pl.BlockSpec(memory_space=pl.ANY)
    return pl.pallas_call(
        functools.partial(kernel, nt, nz),
        out_shape=jax.ShapeDtypeStruct((1, rows, cols), jnp.float32),
        in_specs=[hbm] * 4 + [pl.BlockSpec(memory_space=pltpu.SMEM)],
        out_specs=pl.BlockSpec(memory_space=pltpu.VMEM),
        scratch_shapes=[
            vmem((rows, cols)),
            vmem((3, 2, rows, LANES)),
            vmem((nt, rows, LANES)),
            vmem((3, TALL, LANES)),
            vmem((nt + 1, TALL, LANES)),
            vmem((3, TRIM, LANES)),
            vmem((4, TALL, LANES)),
            vmem((STEPS, LANES)),
            vmem((nt, TRIM, LANES)),
            vmem((stages - 1, TRIM, LANES)),
            vmem((stages - 1, 3, TRIM, LANES)),
            vmem((nt, rows // 2, LANES)),
            vmem((nt, rows // 2, LANES)),
            dma, dma((3, 2)), dma((nt,)), dma((nt,)), dma((2,)), dma((2,)), dma((2, nt + 1)), dma((2, nt + 1)),
            dma((stages - 1, 3, 3)), dma((stages - 1, 3, 3)), dma((nt,)), dma((nt,)),
        ],
        compiler_params=pltpu.CompilerParams(collective_id=0, has_side_effects=True, vmem_limit_bytes=32 * 2**20),
    )(initial_state, guesses, diffusivity, forcing_field, amplitudes)


def solution(mesh):
    placed = (P("space", None), P("tm", "space", None), P("space", None), P("space", None), P("tm"))
    return jax.shard_map(
        per_device, mesh=mesh, in_specs=placed, out_specs=P("tm", "space", None), check_vma=False
    )
```

```python
import functools

import jax
import jax.numpy as jnp
from jax import lax
from jax.experimental import pallas as pl
from jax.experimental.pallas import tpu as pltpu
from jax.sharding import PartitionSpec as P

MESH = pl.DeviceIdType.MESH
ADVECT = 0.01
LANES = 128
STEPS = 8
SPAN = 16
ROWS = 32
HALO = STEPS + SPAN
TALL = ROWS + 2 * HALO
TRIM = TALL - 2 * STEPS
GROUP = 8
BLOCK = 6
SIDE = 32
OWN = LANES - 2 * SIDE


def spans(slabs):
    found = []
    for first in range(0, slabs, SPAN):
        for place in range(SPAN):
            width = (STEPS + SPAN - 1 - place + 7) // 8 * 8
            if found and found[-1][2] == width and place:
                found[-1][1] = first + place + 1
            else:
                found.append([first + place, first + place + 1, width])
    return found


def lanes_of(shape):
    return lax.broadcasted_iota(jnp.int32, shape, 1)


def kernel(
    nt, nz, initial_hbm, guess_hbm, kappa_hbm, forcing_hbm, amp_hbm, out_ref,
    amp_ref, guess, pairs, windows, params, states, coarse, fine, amps, here, there, residual, error, edges, packed, arrived,
    amp_sem, load_sem, pair_sem, win_send, win_recv, par_send, par_recv, z_send, z_recv, edge_send, edge_recv, back_send, back_recv,
):
    tm, z = lax.axis_index("tm"), lax.axis_index("space")
    tiles = guess.shape[1] // LANES
    widths = spans(nt)
    has_up, has_down = z > 0, z < nz - 1
    before, after = lax.rem(tm + nt - 1, nt), lax.rem(tm + 1, nt)

    barrier = pltpu.get_barrier_semaphore()

    def greet(t, where):
        pl.semaphore_signal(barrier, inc=1, device_id=(t, where), device_id_type=MESH)

    def greet_plane(k, carry):
        greet(lax.rem(tm + k, nt), z)
        return carry

    lax.fori_loop(1, nt, greet_plane, 0)

    @pl.when(has_up)
    def _():
        for t in (tm, before, after):
            greet(t, z - 1)

    @pl.when(has_down)
    def _():
        for t in (tm, before, after):
            greet(t, z + 1)

    load_guess = pltpu.make_async_copy(guess_hbm.at[0], guess, load_sem)
    load_guess.start()
    load_amps = pltpu.make_async_copy(amp_hbm, amp_ref, amp_sem)
    load_amps.start()
    first = lax.rem(lax.div(tm + nt - 1, 2), tiles)
    second = lax.rem(first + 1, tiles)
    loads = []
    for i, ref in enumerate((initial_hbm, kappa_hbm, forcing_hbm)):
        for k, tile in enumerate((first, second)):
            columns = pl.ds(pl.multiple_of(tile * LANES, LANES), LANES)
            loads.append(pltpu.make_async_copy(ref.at[:, columns], pairs.at[i, k], pair_sem.at[i, k]))
    for load in loads:
        load.start()

    def state_rows(t, first, count):
        return pl.ds(pl.multiple_of(t * TALL + first, 8), count)

    def clear(first, t, carry):
        states[state_rows(t, first, HALO), :] = jnp.zeros((HALO, LANES), jnp.float32)
        return carry

    @pl.when(jnp.logical_not(has_up))
    def _():
        params[:, :HALO, :] = jnp.zeros((3, HALO, LANES), jnp.float32)
        lax.fori_loop(0, nt + 1, functools.partial(clear, 0), 0)

    @pl.when(jnp.logical_not(has_down))
    def _():
        params[:, HALO + ROWS :, :] = jnp.zeros((3, HALO, LANES), jnp.float32)
        lax.fori_loop(0, nt + 1, functools.partial(clear, HALO + ROWS), 0)

    row_index = lax.broadcasted_iota(jnp.int32, (ROWS, LANES), 0)
    lane = lanes_of((ROWS, LANES))
    marks = jnp.zeros((ROWS, LANES), jnp.float32)
    load_amps.wait()
    for k in range(STEPS):
        marks = jnp.where(row_index == k, amp_ref[k], marks)
    marked = (lane == 0) & (row_index < STEPS)

    load_guess.wait()

    def tile_of(i):
        return guess[:, pl.ds(pl.multiple_of(i * LANES, LANES), LANES)]

    def cut(i, carry):
        low, mid, high = (tile_of(lax.rem(i + d, tiles)) for d in (tiles - 1, 0, 1))
        even = jnp.where(lane < SIDE, pltpu.roll(low, SIDE, 1), pltpu.roll(mid, SIDE, 1))
        odd = jnp.where(lane < LANES - SIDE, pltpu.roll(mid, LANES - SIDE, 1), pltpu.roll(high, LANES - SIDE, 1))
        windows[2 * i] = jnp.where(marked, marks, even)
        windows[2 * i + 1] = jnp.where(marked, marks, odd)
        return carry

    lax.fori_loop(0, tiles, cut, 0)
    pl.semaphore_wait(barrier, nt - 1 + 3 * has_up.astype(jnp.int32) + 3 * has_down.astype(jnp.int32))

    def window_copy(source, target):
        return pltpu.make_async_remote_copy(
            windows.at[target], states.at[state_rows(source + 1, HALO, ROWS)], win_send.at[target], win_recv.at[source],
            device_id=(target, z), device_id_type=MESH,
        )

    def send_window(k, carry):
        window_copy(tm, lax.rem(tm + k, nt)).start()
        return carry

    lax.fori_loop(1, nt, send_window, 0)
    states[state_rows(tm + 1, HALO, ROWS), :] = windows[tm]

    for load in loads:
        load.wait()
    shift = jnp.where(lax.rem(tm, 2) == 0, SIDE, LANES - SIDE)
    for i in range(3):
        low, high = pltpu.roll(pairs[i, 0], shift, 1), pltpu.roll(pairs[i, 1], shift, 1)
        value = jnp.where(lane < shift, low, high)
        if i == 0:
            states[HALO : HALO + ROWS, :] = value
        params[i, HALO : HALO + ROWS, :] = value

    def params_up():
        return pltpu.make_async_remote_copy(
            params.at[:, pl.ds(HALO, HALO)], params.at[:, pl.ds(HALO + ROWS, HALO)], par_send.at[0], par_recv.at[0],
            device_id=(tm, z - 1), device_id_type=MESH,
        )

    def params_down():
        return pltpu.make_async_remote_copy(
            params.at[:, pl.ds(ROWS, HALO)], params.at[:, pl.ds(0, HALO)], par_send.at[1], par_recv.at[1],
            device_id=(tm, z + 1), device_id_type=MESH,
        )

    def state_up(t, width):
        return pltpu.make_async_remote_copy(
            states.at[state_rows(t, HALO, width)], states.at[state_rows(t, HALO + ROWS, width)], z_send.at[0, t], z_recv.at[0, t],
            device_id=(tm, z - 1), device_id_type=MESH,
        )

    def state_down(t, width):
        return pltpu.make_async_remote_copy(
            states.at[state_rows(t, HALO + ROWS - width, width)], states.at[state_rows(t, HALO - width, width)], z_send.at[1, t], z_recv.at[1, t],
            device_id=(tm, z + 1), device_id_type=MESH,
        )

    @pl.when(has_up)
    def _():
        params_up().start()

    @pl.when(has_down)
    def _():
        params_down().start()

    def forward(width, t, carry):
        @pl.when(t != tm + 1)
        def _():
            window_copy(t - 1, tm).wait_recv()

        @pl.when(has_up)
        def _():
            state_up(t, width).start()

        @pl.when(has_down)
        def _():
            state_down(t, width).start()

        return carry

    for first, last, width in widths:
        lax.fori_loop(max(first, 1), last, functools.partial(forward, width), 0)

    @pl.when(tm != nt - 1)
    def _():
        window_copy(nt - 1, tm).wait_recv()

    @pl.when(has_down)
    def _():
        params_up().wait_recv()

    @pl.when(has_up)
    def _():
        params_down().wait_recv()

    states[:HALO, :] = params[0, :HALO, :]
    states[HALO + ROWS : TALL, :] = params[0, HALO + ROWS :, :]
    rows = lax.broadcasted_iota(jnp.int32, (TALL, LANES), 0)
    inside = ((rows >= HALO) | has_up) & ((rows < HALO + ROWS) | has_down)

    def factors(factor):
        kappa = params[1]
        centre = jnp.where(inside, 1.0 - factor * (4.0 * kappa + 2.0 * ADVECT), 0.0)
        return centre, jnp.where(inside, factor * (kappa + ADVECT), 0.0), jnp.where(inside, factor * kappa, 0.0)

    for i, value in enumerate(factors(1.0) + (jnp.where(inside, params[2], 0.0),)):
        fine[i] = jnp.broadcast_to(value[:, None, :], (TALL, GROUP, LANES))
    for i, value in enumerate(factors(float(STEPS))):
        coarse[i] = value[STEPS : STEPS + TRIM]

    def arrive(width, t, carry):
        @pl.when(has_down)
        def _():
            state_up(t, width).wait_recv()

        @pl.when(has_up)
        def _():
            state_down(t, width).wait_recv()

        return carry

    def slabs_at(t, r):
        return states[pl.ds(t * TALL + r, GROUP, stride=TALL), :]

    def fine_step(source, target, k, low, high):
        amp = amps[k]
        for r in range(low, high, BLOCK):
            end = min(r + BLOCK, high)
            u = source[r - 1 : end + 1]
            mid = u[1:-1]
            up_left = u[:-2] + pltpu.roll(mid, 1, 2)
            down_right = u[2:] + pltpu.roll(mid, LANES - 1, 2)
            target[r:end] = fine[0, r:end] * mid + fine[1, r:end] * up_left + fine[2, r:end] * down_right + amp * fine[3, r:end]

    def relax(group, edge):
        t = group * GROUP
        for k in range(STEPS):
            amps[k] = jnp.broadcast_to(slabs_at(t + 1, HALO + k)[:, 0:1], (GROUP, LANES))
        for r in range(edge, TALL - edge):
            here[r] = slabs_at(t, r)

        def two_steps(k, carry):
            fine_step(here, there, 2 * k, edge + 1, TALL - edge - 1)
            fine_step(there, here, 2 * k + 1, edge + 1, TALL - edge - 1)
            return carry

        lax.fori_loop(0, STEPS // 2, two_steps, 0)
        for r in range(edge + STEPS, TALL - edge - STEPS):
            residual[group, (r - STEPS) * GROUP : (r - STEPS + 1) * GROUP] = here[r] - slabs_at(t + 1, r)

    def back_copy(source, target):
        return pltpu.make_async_remote_copy(
            packed.at[target], arrived.at[source], back_send.at[target], back_recv.at[source],
            device_id=(target, z), device_id_type=MESH,
        )

    half = ROWS // 2
    lane_half = lanes_of((half, LANES))

    def coarse_at(i):
        return jnp.stack([coarse[i, pl.ds(b, 8, stride=8), :] for b in range(8)])

    def sweep(group, place, e):
        t = group * GROUP + place
        up = jnp.concatenate([pltpu.roll(e[-1:], 1, 1), e[:-1]], axis=0)
        down = jnp.concatenate([e[1:], pltpu.roll(e[:1], 7, 1)], axis=0)
        add = jnp.stack([residual[group, pl.ds(b * GROUP + place, 8, stride=8 * GROUP), :] for b in range(8)])
        e = coarse_at(0) * e + coarse_at(1) * (up + pltpu.roll(e, 1, 2)) + coarse_at(2) * (down + pltpu.roll(e, LANES - 1, 2)) + add
        for b in range(8):
            error[t, pl.ds(b, 8, stride=8), :] = e[b]
        both = jnp.where(
            lane_half < OWN,
            pltpu.roll(error[t, SPAN : SPAN + half, :], LANES - SIDE, 1),
            pltpu.roll(error[t, SPAN + half : SPAN + ROWS, :], SIDE, 1),
        )

        @pl.when(t == tm)
        def _():
            arrived[t] = both

        @pl.when(t != tm)
        def _():
            packed[t] = both
            back_copy(tm, t).start()

        return e

    edge_rows = {-1: (pl.ds(SPAN, SPAN), pl.ds(SPAN + ROWS, SPAN)), 1: (pl.ds(ROWS, SPAN), pl.ds(0, SPAN)), 0: (pl.ds(SPAN, ROWS), pl.ds(SPAN, ROWS))}

    def edge_copies(s):
        for dz in (-1, 0, 1):
            for slot, target in ((2, before), (1, tm), (0, after)):
                if dz == 0 and slot == 1:
                    continue
                rows_here, rows_there = edge_rows[dz]
                copy = pltpu.make_async_remote_copy(
                    error.at[(s + 1) * SPAN - 1, rows_here], edges.at[s, slot, rows_there], edge_send.at[s, slot, dz + 1], edge_recv.at[s, slot, dz + 1],
                    device_id=(target, z + dz), device_id_type=MESH,
                )
                yield dz, copy

    def when_dz(dz, send, do):
        if dz == 0:
            do()
        else:
            up = (dz == -1) == send
            pl.when(has_up if up else has_down)(do)

    stages = nt // SPAN
    lane_trim = lanes_of((TRIM, LANES))
    row_trim = lax.broadcasted_iota(jnp.int32, (TRIM, LANES), 0)
    centre = (row_trim >= SPAN) & (row_trim < SPAN + ROWS)

    e = jnp.zeros((8, 8, LANES), jnp.float32)
    for s in range(stages):
        for first, last, width in widths:
            first, last = max(first, s * SPAN + 1), min(last, (s + 1) * SPAN + 1)
            if first < last:
                lax.fori_loop(first, last, functools.partial(arrive, width), 0)
        for part in range(SPAN // GROUP):
            relax(s * (SPAN // GROUP) + part, part * GROUP)
        if s > 0:
            for dz, copy in edge_copies(s - 1):
                when_dz(dz, False, copy.wait_recv)
            left = pltpu.roll(edges[s - 1, 0], OWN, 1)
            right = pltpu.roll(edges[s - 1, 2], OWN, 1)
            own = jnp.where(centre, error[s * SPAN - 1], edges[s - 1, 1])
            edges[s - 1, 1] = jnp.where(lane_trim < SIDE, left, jnp.where(lane_trim >= LANES - SIDE, right, own))
            e = jnp.stack([edges[s - 1, 1, pl.ds(b, 8, stride=8), :] for b in range(8)])
        for part in range(SPAN // GROUP):
            e = lax.fori_loop(0, GROUP, functools.partial(sweep, s * (SPAN // GROUP) + part), e)
        if s < stages - 1:
            for slot in range(3):
                @pl.when(jnp.logical_not(has_up))
                def _():
                    edges[s, slot, :SPAN, :] = jnp.zeros((SPAN, LANES), jnp.float32)

                @pl.when(jnp.logical_not(has_down))
                def _():
                    edges[s, slot, SPAN + ROWS :, :] = jnp.zeros((SPAN, LANES), jnp.float32)

            for dz, copy in edge_copies(s):
                when_dz(dz, True, copy.start)

    def sent(k, carry):
        window_copy(tm, lax.rem(tm + k, nt)).wait_send()
        return carry

    lax.fori_loop(1, nt, sent, 0)

    def drain(copy, first, last, width):
        lax.fori_loop(max(first, 1), last, lambda t, carry: (copy(t, width).wait_send(), carry)[1], 0)

    @pl.when(has_up)
    def _():
        params_up().wait_send()
        for span in widths:
            drain(state_up, *span)

    @pl.when(has_down)
    def _():
        params_down().wait_send()
        for span in widths:
            drain(state_down, *span)

    for s in range(stages - 1):
        for dz, copy in edge_copies(s):
            when_dz(dz, True, copy.wait_send)

    def collect(k, carry):
        back_copy(lax.rem(tm + k, nt), tm).wait_recv()
        back_copy(tm, lax.rem(tm + k, nt)).wait_send()
        return carry

    lax.fori_loop(1, nt, collect, 0)

    def join(i, carry):
        first, second = arrived[2 * i], arrived[2 * i + 1]
        columns = pl.ds(pl.multiple_of(i * LANES, LANES), LANES)
        top = jnp.where(lane_half < OWN, first, pltpu.roll(second, OWN, 1))
        bottom = jnp.where(lane_half < OWN, pltpu.roll(first, OWN, 1), second)
        out_ref[0, :half, columns] = guess[:half, columns] + top
        out_ref[0, half:, columns] = guess[half:, columns] + bottom
        return carry

    lax.fori_loop(0, tiles, join, 0)


def per_device(initial_state, guesses, diffusivity, forcing_field, amplitudes):
    nt, nz = lax.axis_size("tm"), lax.axis_size("space")
    rows, cols = initial_state.shape
    stages = nt // SPAN
    dma = pltpu.SemaphoreType.DMA
    vmem = functools.partial(pltpu.VMEM, dtype=jnp.float32)
    hbm = pl.BlockSpec(memory_space=pl.ANY)
    return pl.pallas_call(
        functools.partial(kernel, nt, nz),
        out_shape=jax.ShapeDtypeStruct((1, rows, cols), jnp.float32),
        in_specs=[hbm] * 5,
        out_specs=pl.BlockSpec(memory_space=pltpu.VMEM),
        scratch_shapes=[
            pltpu.SMEM((STEPS,), jnp.float32),
            vmem((rows, cols)),
            vmem((3, 2, rows, LANES)),
            vmem((nt, rows, LANES)),
            vmem((3, TALL, LANES)),
            vmem(((nt + 1) * TALL, LANES)),
            vmem((3, TRIM, LANES)),
            vmem((4, TALL, GROUP, LANES)),
            vmem((STEPS, GROUP, LANES)),
            vmem((TALL, GROUP, LANES)),
            vmem((TALL, GROUP, LANES)),
            vmem((nt // GROUP, TRIM * GROUP, LANES)),
            vmem((nt, TRIM, LANES)),
            vmem((stages - 1, 3, TRIM, LANES)),
            vmem((nt, rows // 2, LANES)),
            vmem((nt, rows // 2, LANES)),
            dma, dma, dma((3, 2)), dma((nt,)), dma((nt,)), dma((2,)), dma((2,)), dma((2, nt + 1)), dma((2, nt + 1)),
            dma((stages - 1, 3, 3)), dma((stages - 1, 3, 3)), dma((nt,)), dma((nt,)),
        ],
        compiler_params=pltpu.CompilerParams(collective_id=0, has_side_effects=True, vmem_limit_bytes=60 * 2**20),
    )(initial_state, guesses, diffusivity, forcing_field, amplitudes)


def solution(mesh):
    placed = (P("space", None), P("tm", "space", None), P("space", None), P("space", None), P("tm"))
    return jax.shard_map(
        per_device, mesh=mesh, in_specs=placed, out_specs=P("tm", "space", None), check_vma=False
    )
```

```python
import functools

import jax
import jax.numpy as jnp
from jax import lax
from jax.experimental import pallas as pl
from jax.experimental.pallas import tpu as pltpu
from jax.sharding import PartitionSpec as P

MESH = pl.DeviceIdType.MESH
ADVECT = 0.01
LANES = 128
STEPS = 8
SPAN = 16
ROWS = 32
HALO = STEPS + SPAN
TALL = ROWS + 2 * HALO
TRIM = TALL - 2 * STEPS
GROUP = 8
BLOCK = 6
SIDE = 32
OWN = LANES - 2 * SIDE


def width_of(place):
    return (STEPS + SPAN - 1 - place + 7) // 8 * 8


def spans():
    found = []
    for place in range(SPAN):
        if found and found[-1][2] == width_of(place):
            found[-1][1] = place + 1
        else:
            found.append([place, place + 1, width_of(place)])
    return found


def lanes_of(shape):
    return lax.broadcasted_iota(jnp.int32, shape, 1)


def kernel(
    nt, nz, initial_hbm, guess_hbm, kappa_hbm, forcing_hbm, amp_hbm, out_ref,
    amp_ref, guess, pairs, windows, params, states, coarse, fine, amps, here, there, residual, error, edges, starts, packed, arrived,
    amp_sem, load_sem, pair_sem, win_send, win_recv, par_send, par_recv, z_send, z_recv, edge_send, edge_recv, back_send, back_recv,
):
    tm, z = lax.axis_index("tm"), lax.axis_index("space")
    tiles = guess.shape[1] // LANES
    widths = spans()
    has_up, has_down = z > 0, z < nz - 1
    before, after = lax.rem(tm + nt - 1, nt), lax.rem(tm + 1, nt)

    barrier = pltpu.get_barrier_semaphore()

    def greet(t, where):
        pl.semaphore_signal(barrier, inc=1, device_id=(t, where), device_id_type=MESH)

    def greet_plane(k, carry):
        greet(lax.rem(tm + k, nt), z)
        return carry

    lax.fori_loop(1, nt, greet_plane, 0)

    @pl.when(has_up)
    def _():
        for t in (tm, before, after):
            greet(t, z - 1)

    @pl.when(has_down)
    def _():
        for t in (tm, before, after):
            greet(t, z + 1)

    load_guess = pltpu.make_async_copy(guess_hbm.at[0], guess, load_sem)
    load_guess.start()
    load_amps = pltpu.make_async_copy(amp_hbm, amp_ref, amp_sem)
    load_amps.start()
    first = lax.rem(lax.div(tm + nt - 1, 2), tiles)
    second = lax.rem(first + 1, tiles)
    loads = []
    for i, ref in enumerate((initial_hbm, kappa_hbm, forcing_hbm)):
        for k, tile in enumerate((first, second)):
            columns = pl.ds(pl.multiple_of(tile * LANES, LANES), LANES)
            loads.append(pltpu.make_async_copy(ref.at[:, columns], pairs.at[i, k], pair_sem.at[i, k]))
    for load in loads:
        load.start()

    def state_rows(t, first, count):
        return pl.ds(pl.multiple_of(t * TALL + first, 8), count)

    def clear(first, t, carry):
        states[state_rows(t, first, HALO), :] = jnp.zeros((HALO, LANES), jnp.float32)
        return carry

    @pl.when(jnp.logical_not(has_up))
    def _():
        params[:, :HALO, :] = jnp.zeros((3, HALO, LANES), jnp.float32)
        lax.fori_loop(0, nt + 1, functools.partial(clear, 0), 0)

    @pl.when(jnp.logical_not(has_down))
    def _():
        params[:, HALO + ROWS :, :] = jnp.zeros((3, HALO, LANES), jnp.float32)
        lax.fori_loop(0, nt + 1, functools.partial(clear, HALO + ROWS), 0)

    @pl.when(jnp.logical_not(has_up))
    def _():
        edges[:, :, :SPAN, :] = jnp.zeros((nt // SPAN - 1, 3, SPAN, LANES), jnp.float32)

    @pl.when(jnp.logical_not(has_down))
    def _():
        edges[:, :, SPAN + ROWS :, :] = jnp.zeros((nt // SPAN - 1, 3, SPAN, LANES), jnp.float32)

    row_index = lax.broadcasted_iota(jnp.int32, (ROWS, LANES), 0)
    lane = lanes_of((ROWS, LANES))
    marks = jnp.zeros((ROWS, LANES), jnp.float32)
    load_amps.wait()
    for k in range(STEPS):
        marks = jnp.where(row_index == k, amp_ref[k], marks)
    marked = (lane == 0) & (row_index < STEPS)

    load_guess.wait()

    def tile_of(i):
        return guess[:, pl.ds(pl.multiple_of(i * LANES, LANES), LANES)]

    def cut(i, carry):
        low, mid, high = (tile_of(lax.rem(i + d, tiles)) for d in (tiles - 1, 0, 1))
        even = jnp.where(lane < SIDE, pltpu.roll(low, SIDE, 1), pltpu.roll(mid, SIDE, 1))
        odd = jnp.where(lane < LANES - SIDE, pltpu.roll(mid, LANES - SIDE, 1), pltpu.roll(high, LANES - SIDE, 1))
        windows[2 * i] = jnp.where(marked, marks, even)
        windows[2 * i + 1] = jnp.where(marked, marks, odd)
        return carry

    lax.fori_loop(0, tiles, cut, 0)
    pl.semaphore_wait(barrier, nt - 1 + 3 * has_up.astype(jnp.int32) + 3 * has_down.astype(jnp.int32))

    def window_copy(source, target):
        return pltpu.make_async_remote_copy(
            windows.at[target], states.at[state_rows(source + 1, HALO, ROWS)], win_send.at[target], win_recv.at[source],
            device_id=(target, z), device_id_type=MESH,
        )

    def send_window(k, carry):
        window_copy(tm, lax.rem(tm + k, nt)).start()
        return carry

    lax.fori_loop(1, nt, send_window, 0)
    states[state_rows(tm + 1, HALO, ROWS), :] = windows[tm]

    for load in loads:
        load.wait()
    shift = jnp.where(lax.rem(tm, 2) == 0, SIDE, LANES - SIDE)
    for i in range(3):
        low, high = pltpu.roll(pairs[i, 0], shift, 1), pltpu.roll(pairs[i, 1], shift, 1)
        value = jnp.where(lane < shift, low, high)
        if i == 0:
            states[HALO : HALO + ROWS, :] = value
        params[i, HALO : HALO + ROWS, :] = value

    def params_up():
        return pltpu.make_async_remote_copy(
            params.at[:, pl.ds(HALO, HALO)], params.at[:, pl.ds(HALO + ROWS, HALO)], par_send.at[0], par_recv.at[0],
            device_id=(tm, z - 1), device_id_type=MESH,
        )

    def params_down():
        return pltpu.make_async_remote_copy(
            params.at[:, pl.ds(ROWS, HALO)], params.at[:, pl.ds(0, HALO)], par_send.at[1], par_recv.at[1],
            device_id=(tm, z + 1), device_id_type=MESH,
        )

    def state_up(t, width):
        return pltpu.make_async_remote_copy(
            states.at[state_rows(t, HALO, width)], states.at[state_rows(t, HALO + ROWS, width)], z_send.at[0, t], z_recv.at[0, t],
            device_id=(tm, z - 1), device_id_type=MESH,
        )

    def state_down(t, width):
        return pltpu.make_async_remote_copy(
            states.at[state_rows(t, HALO + ROWS - width, width)], states.at[state_rows(t, HALO - width, width)], z_send.at[1, t], z_recv.at[1, t],
            device_id=(tm, z + 1), device_id_type=MESH,
        )

    @pl.when(has_up)
    def _():
        params_up().start()

    @pl.when(has_down)
    def _():
        params_down().start()

    def forward(width, t, carry):
        @pl.when(t != tm + 1)
        def _():
            window_copy(t - 1, tm).wait_recv()

        @pl.when(has_up)
        def _():
            state_up(t, width).start()

        @pl.when(has_down)
        def _():
            state_down(t, width).start()

        return carry

    def forward_stage(s, carry):
        for first, last, width in widths:
            lax.fori_loop(jnp.maximum(s * SPAN + first, 1), s * SPAN + last, functools.partial(forward, width), 0)
        return carry

    lax.fori_loop(0, nt // SPAN, forward_stage, 0)

    @pl.when(tm != nt - 1)
    def _():
        window_copy(nt - 1, tm).wait_recv()

    @pl.when(has_down)
    def _():
        params_up().wait_recv()

    @pl.when(has_up)
    def _():
        params_down().wait_recv()

    states[:HALO, :] = params[0, :HALO, :]
    states[HALO + ROWS : TALL, :] = params[0, HALO + ROWS :, :]

    def factors(i, carry):
        rows = pl.ds(pl.multiple_of(i * GROUP, GROUP), GROUP)
        row = i * GROUP + lax.broadcasted_iota(jnp.int32, (GROUP, LANES), 0)
        inside = ((row >= HALO) | has_up) & ((row < HALO + ROWS) | has_down)
        kappa = params[1, rows, :]
        for ref, factor in ((fine, 1.0), (coarse, float(STEPS))):
            for k, value in enumerate((1.0 - factor * (4.0 * kappa + 2.0 * ADVECT), factor * (kappa + ADVECT), factor * kappa)):
                value = jnp.where(inside, value, 0.0)
                if ref is fine:
                    fine[k, rows] = jnp.broadcast_to(value[:, None, :], (GROUP, GROUP, LANES))
                else:
                    coarse[k, rows, :] = value
        forcing = jnp.where(inside, params[2, rows, :], 0.0)
        fine[3, rows] = jnp.broadcast_to(forcing[:, None, :], (GROUP, GROUP, LANES))
        return carry

    lax.fori_loop(0, TALL // GROUP, factors, 0)

    def arrive(width, t, carry):
        @pl.when(has_down)
        def _():
            state_up(t, width).wait_recv()

        @pl.when(has_up)
        def _():
            state_down(t, width).wait_recv()

        return carry

    def slabs_at(t, r):
        return states[pl.ds(t * TALL + r, GROUP, stride=TALL), :]

    def fine_step(source, target, k):
        amp = amps[k]
        for r in range(1, TALL - 1, BLOCK):
            end = min(r + BLOCK, TALL - 1)
            u = source[r - 1 : end + 1]
            mid = u[1:-1]
            up_left = u[:-2] + pltpu.roll(mid, 1, 2)
            down_right = u[2:] + pltpu.roll(mid, LANES - 1, 2)
            target[r:end] = fine[0, r:end] * mid + fine[1, r:end] * up_left + fine[2, r:end] * down_right + amp * fine[3, r:end]

    def arrivals(s, parity):
        first = parity * GROUP + 1
        for place in range(first, first + GROUP):
            width = width_of(place % SPAN)
            if place > first and width == width_of((place - 1) % SPAN):
                continue
            last = place
            while last < first + GROUP and width_of(last % SPAN) == width:
                last += 1
            lax.fori_loop(s * SPAN + place, jnp.minimum(s * SPAN + last, nt), functools.partial(arrive, width), 0)

    def relax(group, carry):
        t = group * GROUP
        for parity in range(SPAN // GROUP):
            pl.when(lax.rem(group, SPAN // GROUP) == parity)(functools.partial(arrivals, lax.div(t, SPAN), parity))

        def load_amp(k, carry):
            amps[k] = jnp.broadcast_to(slabs_at(t + 1, HALO + k)[:, 0:1], (GROUP, LANES))
            return carry

        lax.fori_loop(0, STEPS, load_amp, 0, unroll=2)

        def load_rows(i, carry):
            for r in range(GROUP):
                here[i * GROUP + r] = slabs_at(t, i * GROUP + r)
            return carry

        lax.fori_loop(0, TALL // GROUP, load_rows, 0)

        def two_steps(k, carry):
            fine_step(here, there, 2 * k)
            fine_step(there, here, 2 * k + 1)
            return carry

        lax.fori_loop(0, STEPS // 2, two_steps, 0)

        def finish(i, carry):
            for r in range(GROUP):
                row = i * GROUP + r
                residual[group, pl.ds(pl.multiple_of(row * GROUP, GROUP), GROUP), :] = here[STEPS + row] - slabs_at(t + 1, STEPS + row)
            return carry

        lax.fori_loop(0, TRIM // GROUP, finish, 0)
        return carry

    def back_copy(source, target):
        return pltpu.make_async_remote_copy(
            packed.at[target], arrived.at[source], back_send.at[target], back_recv.at[source],
            device_id=(target, z), device_id_type=MESH,
        )

    half = ROWS // 2
    lane_half = lanes_of((half, LANES))

    def sweep(group, e):
        centre, c_up, c_down = ([coarse[i, pl.ds(STEPS + b, 8, stride=8), :] for b in range(8)] for i in range(3))

        def step(place, e):
            t = group * GROUP + place
            above = [pltpu.roll(e[7], 1, 0)] + e[:7]
            below = e[1:] + [pltpu.roll(e[0], 7, 0)]
            after = []
            for b in range(8):
                up_left = above[b] + pltpu.roll(e[b], 1, 1)
                down_right = below[b] + pltpu.roll(e[b], LANES - 1, 1)
                add = residual[group, pl.ds(b * GROUP + place, 8, stride=8 * GROUP), :]
                after.append(centre[b] * e[b] + c_up[b] * up_left + c_down[b] * down_right + add)
            for b in range(8):
                error[t, pl.ds(b, 8, stride=8), :] = after[b]
            return after

        e = lax.fori_loop(0, GROUP, step, e, unroll=2)

        def pack(place, carry):
            t = group * GROUP + place
            top, bottom = error[t, SPAN : SPAN + half, :], error[t, SPAN + half : SPAN + ROWS, :]
            packed[t] = jnp.where(lane_half < OWN, pltpu.roll(top, LANES - SIDE, 1), pltpu.roll(bottom, SIDE, 1))
            return carry

        lax.fori_loop(0, GROUP, pack, 0, unroll=4)

        def give(t, carry):
            @pl.when(t != tm)
            def _():
                back_copy(tm, t).start()

            return carry

        lax.fori_loop(group * GROUP, (group + 1) * GROUP, give, 0)
        return e

    edge_rows = {-1: (pl.ds(SPAN, SPAN), pl.ds(SPAN + ROWS, SPAN)), 1: (pl.ds(ROWS, SPAN), pl.ds(0, SPAN)), 0: (pl.ds(SPAN, ROWS), pl.ds(SPAN, ROWS))}

    def edge_copies(s):
        for dz in (-1, 0, 1):
            for slot, target in ((2, before), (1, tm), (0, after)):
                if dz == 0 and slot == 1:
                    continue
                rows_here, rows_there = edge_rows[dz]
                copy = pltpu.make_async_remote_copy(
                    error.at[(s + 1) * SPAN - 1, rows_here], edges.at[s, slot, rows_there], edge_send.at[s, slot, dz + 1], edge_recv.at[s, slot, dz + 1],
                    device_id=(target, z + dz), device_id_type=MESH,
                )
                yield dz, copy

    def when_dz(dz, send, do):
        if dz == 0:
            do()
        else:
            up = (dz == -1) == send
            pl.when(has_up if up else has_down)(do)

    stages = nt // SPAN
    lane_trim = lanes_of((TRIM, LANES))
    row_trim = lax.broadcasted_iota(jnp.int32, (TRIM, LANES), 0)
    centre = (row_trim >= SPAN) & (row_trim < SPAN + ROWS)

    groups = SPAN // GROUP
    starts[...] = jnp.zeros((TRIM, LANES), jnp.float32)

    def stage(s, carry):
        lax.fori_loop(s * groups, (s + 1) * groups, relax, 0)

        @pl.when(s > 0)
        def _():
            for dz, copy in edge_copies(s - 1):
                when_dz(dz, False, copy.wait_recv)
            left = pltpu.roll(edges[s - 1, 0], OWN, 1)
            right = pltpu.roll(edges[s - 1, 2], OWN, 1)
            own = jnp.where(centre, error[s * SPAN - 1], edges[s - 1, 1])
            starts[...] = jnp.where(lane_trim < SIDE, left, jnp.where(lane_trim >= LANES - SIDE, right, own))

        e = [starts[pl.ds(b, 8, stride=8), :] for b in range(8)]
        lax.fori_loop(s * groups, (s + 1) * groups, sweep, e)

        @pl.when(s < stages - 1)
        def _():
            for dz, copy in edge_copies(s):
                when_dz(dz, True, copy.start)

        return carry

    lax.fori_loop(0, stages, stage, 0)

    def sent(k, carry):
        window_copy(tm, lax.rem(tm + k, nt)).wait_send()
        return carry

    lax.fori_loop(1, nt, sent, 0)

    def drain(copy):
        def drain_stage(s, carry):
            for first, last, width in widths:
                lax.fori_loop(
                    jnp.maximum(s * SPAN + first, 1), s * SPAN + last, lambda t, carry: (copy(t, width).wait_send(), carry)[1], 0
                )
            return carry

        lax.fori_loop(0, nt // SPAN, drain_stage, 0)

    @pl.when(has_up)
    def _():
        params_up().wait_send()
        drain(state_up)

    @pl.when(has_down)
    def _():
        params_down().wait_send()
        drain(state_down)

    for s in range(stages - 1):
        for dz, copy in edge_copies(s):
            when_dz(dz, True, copy.wait_send)

    def collect(k, carry):
        back_copy(lax.rem(tm + k, nt), tm).wait_recv()
        back_copy(tm, lax.rem(tm + k, nt)).wait_send()
        return carry

    lax.fori_loop(1, nt, collect, 0)

    def join(i, carry):
        first, second = arrived[2 * i], arrived[2 * i + 1]
        columns = pl.ds(pl.multiple_of(i * LANES, LANES), LANES)
        top = jnp.where(lane_half < OWN, first, pltpu.roll(second, OWN, 1))
        bottom = jnp.where(lane_half < OWN, pltpu.roll(first, OWN, 1), second)
        out_ref[0, :half, columns] = guess[:half, columns] + top
        out_ref[0, half:, columns] = guess[half:, columns] + bottom
        return carry

    arrived[tm] = packed[tm]
    lax.fori_loop(0, tiles, join, 0, unroll=4)


def per_device(initial_state, guesses, diffusivity, forcing_field, amplitudes):
    nt, nz = lax.axis_size("tm"), lax.axis_size("space")
    rows, cols = initial_state.shape
    stages = nt // SPAN
    dma = pltpu.SemaphoreType.DMA
    vmem = functools.partial(pltpu.VMEM, dtype=jnp.float32)
    hbm = pl.BlockSpec(memory_space=pl.ANY)
    return pl.pallas_call(
        functools.partial(kernel, nt, nz),
        out_shape=jax.ShapeDtypeStruct((1, rows, cols), jnp.float32),
        in_specs=[hbm] * 5,
        out_specs=pl.BlockSpec(memory_space=pltpu.VMEM),
        scratch_shapes=[
            pltpu.SMEM((STEPS,), jnp.float32),
            vmem((rows, cols)),
            vmem((3, 2, rows, LANES)),
            vmem((nt, rows, LANES)),
            vmem((3, TALL, LANES)),
            vmem(((nt + 1) * TALL, LANES)),
            vmem((3, TALL, LANES)),
            vmem((4, TALL, GROUP, LANES)),
            vmem((STEPS, GROUP, LANES)),
            vmem((TALL, GROUP, LANES)),
            vmem((TALL, GROUP, LANES)),
            vmem((nt // GROUP, TRIM * GROUP, LANES)),
            vmem((nt, TRIM, LANES)),
            vmem((stages - 1, 3, TRIM, LANES)),
            vmem((TRIM, LANES)),
            vmem((nt, rows // 2, LANES)),
            vmem((nt, rows // 2, LANES)),
            dma, dma, dma((3, 2)), dma((nt,)), dma((nt,)), dma((2,)), dma((2,)), dma((2, nt + 1)), dma((2, nt + 1)),
            dma((stages - 1, 3, 3)), dma((stages - 1, 3, 3)), dma((nt,)), dma((nt,)),
        ],
        compiler_params=pltpu.CompilerParams(collective_id=0, has_side_effects=True, vmem_limit_bytes=60 * 2**20),
    )(initial_state, guesses, diffusivity, forcing_field, amplitudes)


def solution(mesh):
    placed = (P("space", None), P("tm", "space", None), P("space", None), P("space", None), P("tm"))
    return jax.shard_map(
        per_device, mesh=mesh, in_specs=placed, out_specs=P("tm", "space", None), check_vma=False
    )
```

```python
import functools

import jax
import jax.numpy as jnp
from jax import lax
from jax.experimental import pallas as pl
from jax.experimental.pallas import tpu as pltpu
from jax.sharding import PartitionSpec as P

MESH = pl.DeviceIdType.MESH
ADVECT = 0.01
LANES = 128
STEPS = 8
SPAN = 16
ROWS = 32
HALO = STEPS + SPAN
TALL = ROWS + 2 * HALO
TRIM = TALL - 2 * STEPS
GROUP = 8
PAIR = SPAN // GROUP
CORE = ROWS - 2 * STEPS
BLOCK = 6
SIDE = 32
OWN = LANES - 2 * SIDE


def width_of(place):
    return (STEPS + SPAN - 1 - place + 7) // 8 * 8


def spans():
    found = []
    for place in range(SPAN):
        if found and found[-1][2] == width_of(place):
            found[-1][1] = place + 1
        else:
            found.append([place, place + 1, width_of(place)])
    return found


def lanes_of(shape):
    return lax.broadcasted_iota(jnp.int32, shape, 1)


def kernel(
    nt, nz, initial_hbm, guess_hbm, kappa_hbm, forcing_hbm, amp_hbm, out_ref,
    amp_ref, guess, pairs, windows, params, body, high, low, coarse, fine, amps, inner, inner_next, border, core, outer, outer_next, residual, error, edges, starts, packed, arrived,
    amp_sem, load_sem, pair_sem, win_send, win_recv, par_send, par_recv, z_send, z_recv, edge_send, edge_recv, back_send, back_recv,
):
    tm, z = lax.axis_index("tm"), lax.axis_index("space")
    tiles = guess.shape[1] // LANES
    widths = spans()
    has_up, has_down = z > 0, z < nz - 1
    before, after = lax.rem(tm + nt - 1, nt), lax.rem(tm + 1, nt)

    barrier = pltpu.get_barrier_semaphore()

    def greet(t, where):
        pl.semaphore_signal(barrier, inc=1, device_id=(t, where), device_id_type=MESH)

    def greet_plane(k, carry):
        greet(lax.rem(tm + k, nt), z)
        return carry

    lax.fori_loop(1, nt, greet_plane, 0)

    @pl.when(has_up)
    def _():
        for t in (tm, before, after):
            greet(t, z - 1)

    @pl.when(has_down)
    def _():
        for t in (tm, before, after):
            greet(t, z + 1)

    load_guess = pltpu.make_async_copy(guess_hbm.at[0], guess, load_sem)
    load_guess.start()
    load_amps = pltpu.make_async_copy(amp_hbm, amp_ref, amp_sem)
    load_amps.start()
    first = lax.rem(lax.div(tm + nt - 1, 2), tiles)
    second = lax.rem(first + 1, tiles)
    loads = []
    for i, ref in enumerate((initial_hbm, kappa_hbm, forcing_hbm)):
        for k, tile in enumerate((first, second)):
            columns = pl.ds(pl.multiple_of(tile * LANES, LANES), LANES)
            loads.append(pltpu.make_async_copy(ref.at[:, columns], pairs.at[i, k], pair_sem.at[i, k]))
    for load in loads:
        load.start()

    def body_rows(t, first, count):
        return pl.ds(pl.multiple_of(t * ROWS + first, 8), count)

    def halo_rows(t, first, count):
        return pl.ds(pl.multiple_of(t * HALO + first, 8), count)

    def clear(ref, t, carry):
        ref[halo_rows(t, 0, HALO), :] = jnp.zeros((HALO, LANES), jnp.float32)
        return carry

    @pl.when(jnp.logical_not(has_up))
    def _():
        params[:, :HALO, :] = jnp.zeros((3, HALO, LANES), jnp.float32)
        lax.fori_loop(0, nt + 1, functools.partial(clear, high), 0)

    @pl.when(jnp.logical_not(has_down))
    def _():
        params[:, HALO + ROWS :, :] = jnp.zeros((3, HALO, LANES), jnp.float32)
        lax.fori_loop(0, nt + 1, functools.partial(clear, low), 0)

    @pl.when(jnp.logical_not(has_up))
    def _():
        edges[:, :, :SPAN, :] = jnp.zeros((nt // SPAN - 1, 3, SPAN, LANES), jnp.float32)

    @pl.when(jnp.logical_not(has_down))
    def _():
        edges[:, :, SPAN + ROWS :, :] = jnp.zeros((nt // SPAN - 1, 3, SPAN, LANES), jnp.float32)

    row_index = lax.broadcasted_iota(jnp.int32, (ROWS, LANES), 0)
    lane = lanes_of((ROWS, LANES))
    marks = jnp.zeros((ROWS, LANES), jnp.float32)
    load_amps.wait()
    for k in range(STEPS):
        marks = jnp.where(row_index == k, amp_ref[k], marks)
    marked = (lane == 0) & (row_index < STEPS)

    load_guess.wait()

    def tile_of(i):
        return guess[:, pl.ds(pl.multiple_of(i * LANES, LANES), LANES)]

    def cut(i, carry):
        low, mid, high = (tile_of(lax.rem(i + d, tiles)) for d in (tiles - 1, 0, 1))
        even = jnp.where(lane < SIDE, pltpu.roll(low, SIDE, 1), pltpu.roll(mid, SIDE, 1))
        odd = jnp.where(lane < LANES - SIDE, pltpu.roll(mid, LANES - SIDE, 1), pltpu.roll(high, LANES - SIDE, 1))
        windows[2 * i] = jnp.where(marked, marks, even)
        windows[2 * i + 1] = jnp.where(marked, marks, odd)
        return carry

    lax.fori_loop(0, tiles, cut, 0)
    pl.semaphore_wait(barrier, nt - 1 + 3 * has_up.astype(jnp.int32) + 3 * has_down.astype(jnp.int32))

    def window_copy(source, target):
        return pltpu.make_async_remote_copy(
            windows.at[target], body.at[body_rows(source + 1, 0, ROWS)], win_send.at[target], win_recv.at[source],
            device_id=(target, z), device_id_type=MESH,
        )

    def send_window(k, carry):
        window_copy(tm, lax.rem(tm + k, nt)).start()
        return carry

    lax.fori_loop(1, nt, send_window, 0)
    body[body_rows(tm + 1, 0, ROWS), :] = windows[tm]

    for load in loads:
        load.wait()
    shift = jnp.where(lax.rem(tm, 2) == 0, SIDE, LANES - SIDE)
    for i in range(3):
        lower, upper = pltpu.roll(pairs[i, 0], shift, 1), pltpu.roll(pairs[i, 1], shift, 1)
        value = jnp.where(lane < shift, lower, upper)
        if i == 0:
            body[:ROWS, :] = value
        params[i, HALO : HALO + ROWS, :] = value

    def params_up():
        return pltpu.make_async_remote_copy(
            params.at[:, pl.ds(HALO, HALO)], params.at[:, pl.ds(HALO + ROWS, HALO)], par_send.at[0], par_recv.at[0],
            device_id=(tm, z - 1), device_id_type=MESH,
        )

    def params_down():
        return pltpu.make_async_remote_copy(
            params.at[:, pl.ds(ROWS, HALO)], params.at[:, pl.ds(0, HALO)], par_send.at[1], par_recv.at[1],
            device_id=(tm, z + 1), device_id_type=MESH,
        )

    def state_up(t, width):
        return pltpu.make_async_remote_copy(
            body.at[body_rows(t, 0, width)], low.at[halo_rows(t, 0, width)], z_send.at[0, t], z_recv.at[0, t],
            device_id=(tm, z - 1), device_id_type=MESH,
        )

    def state_down(t, width):
        return pltpu.make_async_remote_copy(
            body.at[body_rows(t, ROWS - width, width)], high.at[halo_rows(t, HALO - width, width)], z_send.at[1, t], z_recv.at[1, t],
            device_id=(tm, z + 1), device_id_type=MESH,
        )

    @pl.when(has_up)
    def _():
        params_up().start()

    @pl.when(has_down)
    def _():
        params_down().start()

    def forward(width, t, carry):
        @pl.when(t != tm + 1)
        def _():
            window_copy(t - 1, tm).wait_recv()

        @pl.when(has_up)
        def _():
            state_up(t, width).start()

        @pl.when(has_down)
        def _():
            state_down(t, width).start()

        return carry

    def forward_stage(s, carry):
        for first, last, width in widths:
            lax.fori_loop(jnp.maximum(s * SPAN + first, 1), s * SPAN + last, functools.partial(forward, width), 0)
        return carry

    lax.fori_loop(0, nt // SPAN, forward_stage, 0)

    @pl.when(tm != nt - 1)
    def _():
        window_copy(nt - 1, tm).wait_recv()

    def factors(i):
        rows = pl.ds(pl.multiple_of(i * GROUP, GROUP), GROUP)
        row = i * GROUP + lax.broadcasted_iota(jnp.int32, (GROUP, LANES), 0)
        inside = ((row >= HALO) | has_up) & ((row < HALO + ROWS) | has_down)
        kappa = params[1, rows, :]
        for ref, factor in ((fine, 1.0), (coarse, float(STEPS))):
            for k, value in enumerate((1.0 - factor * (4.0 * kappa + 2.0 * ADVECT), factor * (kappa + ADVECT), factor * kappa)):
                value = jnp.where(inside, value, 0.0)
                if ref is fine:
                    fine[k, rows] = jnp.broadcast_to(value[:, None, :], (GROUP, GROUP, LANES))
                else:
                    coarse[k, rows, :] = value
        forcing = jnp.where(inside, params[2, rows, :], 0.0)
        fine[3, rows] = jnp.broadcast_to(forcing[:, None, :], (GROUP, GROUP, LANES))

    def own_factors(i, carry):
        factors(HALO // GROUP + i)
        return carry

    lax.fori_loop(0, ROWS // GROUP, own_factors, 0)

    def body_at(t, r):
        return body[pl.ds(t * ROWS + r, GROUP, stride=ROWS), :]

    def halo_at(ref, t, r):
        return ref[pl.ds(t * HALO + r, GROUP, stride=HALO), :]

    def advance(load, store, amp, first, count):
        for r in range(0, count, BLOCK):
            n = min(BLOCK, count - r)
            u = load(r, n + 2)
            mid = u[1:-1]
            up_left = u[:-2] + pltpu.roll(mid, 1, 2)
            down_right = u[2:] + pltpu.roll(mid, LANES - 1, 2)
            centre, c_up, c_down, forcing = (fine[i, pl.ds(first + r, n)] for i in range(4))
            store(r, n, centre * mid + c_up * up_left + c_down * down_right + amp * forcing)

    def inner_step(source, target, s, k):
        for g in range(PAIR):
            border[s, g, k, 0:2] = source[g, pl.ds(k, 2)]
            border[s, g, k, 2:4] = source[g, pl.ds(ROWS - 2 - k, 2)]

            def load(r, n):
                return source[g, r : r + n]

            def store(r, n, value):
                target[g, r + 1 : r + 1 + n] = value

            advance(load, store, amps[s, g, k], HALO + 1, ROWS - 2)

    def relax_inner(s, carry):
        for g in range(PAIR):
            t = s * SPAN + g * GROUP

            def load_amp(k, carry):
                amps[s, g, k] = jnp.broadcast_to(body_at(t + 1, k)[:, 0:1], (GROUP, LANES))
                return carry

            lax.fori_loop(0, STEPS, load_amp, 0, unroll=2)

            def load_rows(i, carry):
                for r in range(GROUP):
                    inner[g, i * GROUP + r] = body_at(t, i * GROUP + r)
                return carry

            lax.fori_loop(0, ROWS // GROUP, load_rows, 0)

        def two_steps(k, carry):
            inner_step(inner, inner_next, s, 2 * k)
            inner_step(inner_next, inner, s, 2 * k + 1)
            return carry

        lax.fori_loop(0, STEPS // 2, two_steps, 0)
        for g in range(PAIR):
            core[s, g] = inner[g, STEPS : STEPS + CORE]
        return carry

    lax.fori_loop(0, nt // SPAN, relax_inner, 0)

    @pl.when(has_down)
    def _():
        params_up().wait_recv()

    @pl.when(has_up)
    def _():
        params_down().wait_recv()

    high[:HALO, :] = params[0, :HALO, :]
    low[:HALO, :] = params[0, HALO + ROWS :, :]

    def halo_factors(i, carry):
        factors(jnp.where(i < HALO // GROUP, i, i + ROWS // GROUP))
        return carry

    lax.fori_loop(0, 2 * HALO // GROUP, halo_factors, 0)

    def arrive(width, t, carry):
        @pl.when(has_down)
        def _():
            state_up(t, width).wait_recv()

        @pl.when(has_up)
        def _():
            state_down(t, width).wait_recv()

        return carry

    def arrivals(s):
        for first, last, width in widths:
            lax.fori_loop(s * SPAN + max(first, 1), s * SPAN + last, functools.partial(arrive, width), 0)

        @pl.when(s < nt // SPAN - 1)
        def _():
            arrive(HALO, (s + 1) * SPAN, 0)

    def outer_step(source, target, s, k):
        for g in range(PAIR):
            for side in range(2):
                def load(r, n):
                    if side == 0 and r + n > HALO:
                        return jnp.concatenate([source[g, 0, r:HALO], border[s, g, k, 0 : r + n - HALO]], axis=0)
                    if side == 1 and r < 2:
                        return jnp.concatenate([border[s, g, k, 2 + r : 4], source[g, 1, 0 : r + n - 2]], axis=0)
                    first = r - 2 * side
                    return source[g, side, first : first + n]

                def store(r, n, value):
                    target[g, side, r : r + n] = value

                advance(load, store, amps[s, g, k], k + 1 if side == 0 else HALO + ROWS - 1 - k, HALO)

    def relax(s):
        arrivals(s)
        for g in range(PAIR):
            t = s * SPAN + g * GROUP

            def load_rows(i, carry):
                for r in range(GROUP):
                    outer[g, 0, i * GROUP + r] = halo_at(high, t, i * GROUP + r)
                    outer[g, 1, i * GROUP + r] = halo_at(low, t, i * GROUP + r)
                return carry

            lax.fori_loop(0, HALO // GROUP, load_rows, 0)

        def two_steps(k, carry):
            outer_step(outer, outer_next, s, 2 * k)
            outer_step(outer_next, outer, s, 2 * k + 1)
            return carry

        lax.fori_loop(0, STEPS // 2, two_steps, 0)

        for g in range(PAIR):
            t = s * SPAN + g * GROUP

            def put(row, value):
                residual[s * PAIR + g, pl.ds(pl.multiple_of((row - STEPS) * GROUP, GROUP), GROUP), :] = value

            def finish_halo(i, carry):
                for r in range(GROUP):
                    row = i * GROUP + r
                    put(STEPS + row, outer[g, 0, row] - halo_at(high, t + 1, STEPS + row))
                    put(HALO + ROWS + row, outer[g, 1, STEPS + row] - halo_at(low, t + 1, row))
                return carry

            lax.fori_loop(0, (HALO - STEPS) // GROUP, finish_halo, 0)
            for r in range(STEPS):
                put(HALO + r, outer[g, 0, HALO - STEPS + r] - body_at(t + 1, r))
                put(HALO + ROWS - STEPS + r, outer[g, 1, r] - body_at(t + 1, ROWS - STEPS + r))

            def finish_core(i, carry):
                for r in range(GROUP):
                    row = i * GROUP + r
                    put(HALO + STEPS + row, core[s, g, row] - body_at(t + 1, STEPS + row))
                return carry

            lax.fori_loop(0, CORE // GROUP, finish_core, 0)

    def back_copy(source, target):
        return pltpu.make_async_remote_copy(
            packed.at[target], arrived.at[source], back_send.at[target], back_recv.at[source],
            device_id=(target, z), device_id_type=MESH,
        )

    half = ROWS // 2
    lane_half = lanes_of((half, LANES))

    def sweep(group, e):
        centre, c_up, c_down = ([coarse[i, pl.ds(STEPS + b, 8, stride=8), :] for b in range(8)] for i in range(3))

        def step(place, e):
            t = group * GROUP + place
            above = [pltpu.roll(e[7], 1, 0)] + e[:7]
            below = e[1:] + [pltpu.roll(e[0], 7, 0)]
            after = []
            for b in range(8):
                up_left = above[b] + pltpu.roll(e[b], 1, 1)
                down_right = below[b] + pltpu.roll(e[b], LANES - 1, 1)
                add = residual[group, pl.ds(b * GROUP + place, 8, stride=8 * GROUP), :]
                after.append(centre[b] * e[b] + c_up[b] * up_left + c_down[b] * down_right + add)
            for b in range(8):
                error[t, pl.ds(b, 8, stride=8), :] = after[b]
            return after

        e = lax.fori_loop(0, GROUP, step, e, unroll=2)

        def pack(place, carry):
            t = group * GROUP + place
            top, bottom = error[t, SPAN : SPAN + half, :], error[t, SPAN + half : SPAN + ROWS, :]
            packed[t] = jnp.where(lane_half < OWN, pltpu.roll(top, LANES - SIDE, 1), pltpu.roll(bottom, SIDE, 1))
            return carry

        lax.fori_loop(0, GROUP, pack, 0, unroll=4)

        def give(t, carry):
            @pl.when(t != tm)
            def _():
                back_copy(tm, t).start()

            return carry

        lax.fori_loop(group * GROUP, (group + 1) * GROUP, give, 0)
        return e

    edge_rows = {-1: (pl.ds(SPAN, SPAN), pl.ds(SPAN + ROWS, SPAN)), 1: (pl.ds(ROWS, SPAN), pl.ds(0, SPAN)), 0: (pl.ds(SPAN, ROWS), pl.ds(SPAN, ROWS))}

    def edge_copies(s):
        for dz in (-1, 0, 1):
            for slot, target in ((2, before), (1, tm), (0, after)):
                if dz == 0 and slot == 1:
                    continue
                rows_here, rows_there = edge_rows[dz]
                copy = pltpu.make_async_remote_copy(
                    error.at[(s + 1) * SPAN - 1, rows_here], edges.at[s, slot, rows_there], edge_send.at[s, slot, dz + 1], edge_recv.at[s, slot, dz + 1],
                    device_id=(target, z + dz), device_id_type=MESH,
                )
                yield dz, copy

    def when_dz(dz, send, do):
        if dz == 0:
            do()
        else:
            up = (dz == -1) == send
            pl.when(has_up if up else has_down)(do)

    stages = nt // SPAN
    lane_trim = lanes_of((TRIM, LANES))
    row_trim = lax.broadcasted_iota(jnp.int32, (TRIM, LANES), 0)
    centre = (row_trim >= SPAN) & (row_trim < SPAN + ROWS)

    groups = SPAN // GROUP
    starts[...] = jnp.zeros((TRIM, LANES), jnp.float32)

    def stage(s, carry):
        relax(s)

        @pl.when(s > 0)
        def _():
            for dz, copy in edge_copies(s - 1):
                when_dz(dz, False, copy.wait_recv)
            left = pltpu.roll(edges[s - 1, 0], OWN, 1)
            right = pltpu.roll(edges[s - 1, 2], OWN, 1)
            own = jnp.where(centre, error[s * SPAN - 1], edges[s - 1, 1])
            starts[...] = jnp.where(lane_trim < SIDE, left, jnp.where(lane_trim >= LANES - SIDE, right, own))

        e = [starts[pl.ds(b, 8, stride=8), :] for b in range(8)]
        lax.fori_loop(s * groups, (s + 1) * groups, sweep, e)

        @pl.when(s < stages - 1)
        def _():
            for dz, copy in edge_copies(s):
                when_dz(dz, True, copy.start)

        return carry

    lax.fori_loop(0, stages, stage, 0)

    def sent(k, carry):
        window_copy(tm, lax.rem(tm + k, nt)).wait_send()
        return carry

    lax.fori_loop(1, nt, sent, 0)

    def drain(copy):
        def drain_stage(s, carry):
            for first, last, width in widths:
                lax.fori_loop(
                    jnp.maximum(s * SPAN + first, 1), s * SPAN + last, lambda t, carry: (copy(t, width).wait_send(), carry)[1], 0
                )
            return carry

        lax.fori_loop(0, nt // SPAN, drain_stage, 0)

    @pl.when(has_up)
    def _():
        params_up().wait_send()
        drain(state_up)

    @pl.when(has_down)
    def _():
        params_down().wait_send()
        drain(state_down)

    for s in range(stages - 1):
        for dz, copy in edge_copies(s):
            when_dz(dz, True, copy.wait_send)

    def collect(k, carry):
        back_copy(lax.rem(tm + k, nt), tm).wait_recv()
        back_copy(tm, lax.rem(tm + k, nt)).wait_send()
        return carry

    lax.fori_loop(1, nt, collect, 0)

    def join(i, carry):
        first, second = arrived[2 * i], arrived[2 * i + 1]
        columns = pl.ds(pl.multiple_of(i * LANES, LANES), LANES)
        top = jnp.where(lane_half < OWN, first, pltpu.roll(second, OWN, 1))
        bottom = jnp.where(lane_half < OWN, pltpu.roll(first, OWN, 1), second)
        out_ref[0, :half, columns] = guess[:half, columns] + top
        out_ref[0, half:, columns] = guess[half:, columns] + bottom
        return carry

    arrived[tm] = packed[tm]
    lax.fori_loop(0, tiles, join, 0, unroll=4)


def per_device(initial_state, guesses, diffusivity, forcing_field, amplitudes):
    nt, nz = lax.axis_size("tm"), lax.axis_size("space")
    rows, cols = initial_state.shape
    stages = nt // SPAN
    dma = pltpu.SemaphoreType.DMA
    vmem = functools.partial(pltpu.VMEM, dtype=jnp.float32)
    hbm = pl.BlockSpec(memory_space=pl.ANY)
    return pl.pallas_call(
        functools.partial(kernel, nt, nz),
        out_shape=jax.ShapeDtypeStruct((1, rows, cols), jnp.float32),
        in_specs=[hbm] * 5,
        out_specs=pl.BlockSpec(memory_space=pltpu.VMEM),
        scratch_shapes=[
            pltpu.SMEM((STEPS,), jnp.float32),
            vmem((rows, cols)),
            vmem((3, 2, rows, LANES)),
            vmem((nt, rows, LANES)),
            vmem((3, TALL, LANES)),
            vmem(((nt + 1) * ROWS, LANES)),
            vmem(((nt + 1) * HALO, LANES)),
            vmem(((nt + 1) * HALO, LANES)),
            vmem((3, TALL, LANES)),
            vmem((4, TALL, GROUP, LANES)),
            vmem((nt // SPAN, PAIR, STEPS, GROUP, LANES)),
            vmem((PAIR, ROWS, GROUP, LANES)),
            vmem((PAIR, ROWS, GROUP, LANES)),
            vmem((nt // SPAN, PAIR, STEPS, 4, GROUP, LANES)),
            vmem((nt // SPAN, PAIR, CORE, GROUP, LANES)),
            vmem((PAIR, 2, HALO, GROUP, LANES)),
            vmem((PAIR, 2, HALO, GROUP, LANES)),
            vmem((nt // GROUP, TRIM * GROUP, LANES)),
            vmem((nt, TRIM, LANES)),
            vmem((stages - 1, 3, TRIM, LANES)),
            vmem((TRIM, LANES)),
            vmem((nt, rows // 2, LANES)),
            vmem((nt, rows // 2, LANES)),
            dma, dma, dma((3, 2)), dma((nt,)), dma((nt,)), dma((2,)), dma((2,)), dma((2, nt + 1)), dma((2, nt + 1)),
            dma((stages - 1, 3, 3)), dma((stages - 1, 3, 3)), dma((nt,)), dma((nt,)),
        ],
        compiler_params=pltpu.CompilerParams(collective_id=0, has_side_effects=True, vmem_limit_bytes=60 * 2**20),
    )(initial_state, guesses, diffusivity, forcing_field, amplitudes)


def solution(mesh):
    placed = (P("space", None), P("tm", "space", None), P("space", None), P("space", None), P("tm"))
    return jax.shard_map(
        per_device, mesh=mesh, in_specs=placed, out_specs=P("tm", "space", None), check_vma=False
    )
```

```python
import functools

import jax
import jax.numpy as jnp
from jax import lax
from jax.experimental import pallas as pl
from jax.experimental.pallas import tpu as pltpu
from jax.sharding import PartitionSpec as P

MESH = pl.DeviceIdType.MESH
ADVECT = 0.01
LANES = 128
STEPS = 8
SPAN = 16
ROWS = 32
HALO = STEPS + SPAN
TALL = ROWS + 2 * HALO
TRIM = TALL - 2 * STEPS
GROUP = 8
PAIR = SPAN // GROUP
CORE = ROWS - 2 * STEPS
BLOCK = 6
ACROSS = 8
SIDE = 32
OWN = LANES - 2 * SIDE
VMEM_LIMIT = 536 * 2**20 // 10


def width_of(place):
    return (STEPS + SPAN - 1 - place + 7) // 8 * 8


def spans():
    found = []
    for place in range(SPAN):
        if found and found[-1][2] == width_of(place):
            found[-1][1] = place + 1
        else:
            found.append([place, place + 1, width_of(place)])
    return found


def window_of(device):
    turn = lax.rem(lax.div(device, ACROSS), 2)
    place = lax.rem(device, ACROSS)
    return device - place + jnp.where(turn == 1, ACROSS - 1 - place, place)


def lanes_of(shape):
    return lax.broadcasted_iota(jnp.int32, shape, 1)


def kernel(
    nt, nz, initial_hbm, guess_hbm, kappa_hbm, forcing_hbm, amp_hbm, out_ref,
    amp_ref, guess, pairs, windows, params, body, high, low, coarse, fine, amps, inner, inner_next, border, core, outer, outer_next, residual, error, edges, starts, packed, arrived,
    amp_sem, load_sem, pair_sem, win_send, win_recv, par_send, par_recv, z_send, z_recv, edge_send, edge_recv, back_send, back_recv,
):
    tm, z = lax.axis_index("tm"), lax.axis_index("space")
    tiles = guess.shape[1] // LANES
    widths = spans()
    has_up, has_down = z > 0, z < nz - 1
    mine = window_of(tm)
    before, after = window_of(lax.rem(mine + nt - 1, nt)), window_of(lax.rem(mine + 1, nt))

    barrier = pltpu.get_barrier_semaphore()

    def greet(t, where):
        pl.semaphore_signal(barrier, inc=1, device_id=(t, where), device_id_type=MESH)

    def greet_plane(k, carry):
        greet(lax.rem(tm + k, nt), z)
        return carry

    lax.fori_loop(1, nt, greet_plane, 0)

    @pl.when(has_up)
    def _():
        for t in (tm, before, after):
            greet(t, z - 1)

    @pl.when(has_down)
    def _():
        for t in (tm, before, after):
            greet(t, z + 1)

    load_guess = pltpu.make_async_copy(guess_hbm.at[0], guess, load_sem)
    load_guess.start()
    load_amps = pltpu.make_async_copy(amp_hbm, amp_ref, amp_sem)
    load_amps.start()
    first = lax.rem(lax.div(mine + nt - 1, 2), tiles)
    second = lax.rem(first + 1, tiles)
    loads = []
    for i, ref in enumerate((initial_hbm, kappa_hbm, forcing_hbm)):
        for k, tile in enumerate((first, second)):
            columns = pl.ds(pl.multiple_of(tile * LANES, LANES), LANES)
            loads.append(pltpu.make_async_copy(ref.at[:, columns], pairs.at[i, k], pair_sem.at[i, k]))
    for load in loads:
        load.start()

    def body_rows(t, first, count):
        return pl.ds(pl.multiple_of(t * ROWS + first, 8), count)

    def halo_rows(t, first, count):
        return pl.ds(pl.multiple_of(t * HALO + first, 8), count)

    def clear(ref, t, carry):
        ref[halo_rows(t, 0, HALO), :] = jnp.zeros((HALO, LANES), jnp.float32)
        return carry

    @pl.when(jnp.logical_not(has_up))
    def _():
        params[:, :HALO, :] = jnp.zeros((3, HALO, LANES), jnp.float32)
        lax.fori_loop(0, nt + 1, functools.partial(clear, high), 0)

    @pl.when(jnp.logical_not(has_down))
    def _():
        params[:, HALO + ROWS :, :] = jnp.zeros((3, HALO, LANES), jnp.float32)
        lax.fori_loop(0, nt + 1, functools.partial(clear, low), 0)

    @pl.when(jnp.logical_not(has_up))
    def _():
        edges[:, :, :SPAN, :] = jnp.zeros((nt // SPAN - 1, 3, SPAN, LANES), jnp.float32)

    @pl.when(jnp.logical_not(has_down))
    def _():
        edges[:, :, SPAN + ROWS :, :] = jnp.zeros((nt // SPAN - 1, 3, SPAN, LANES), jnp.float32)

    row_index = lax.broadcasted_iota(jnp.int32, (ROWS, LANES), 0)
    lane = lanes_of((ROWS, LANES))
    marks = jnp.zeros((ROWS, LANES), jnp.float32)
    load_amps.wait()
    for k in range(STEPS):
        marks = jnp.where(row_index == k, amp_ref[k], marks)
    marked = (lane == 0) & (row_index < STEPS)

    load_guess.wait()

    def tile_of(i):
        return guess[:, pl.ds(pl.multiple_of(i * LANES, LANES), LANES)]

    def cut(i, carry):
        low, mid, high = (tile_of(lax.rem(i + d, tiles)) for d in (tiles - 1, 0, 1))
        even = jnp.where(lane < SIDE, pltpu.roll(low, SIDE, 1), pltpu.roll(mid, SIDE, 1))
        odd = jnp.where(lane < LANES - SIDE, pltpu.roll(mid, LANES - SIDE, 1), pltpu.roll(high, LANES - SIDE, 1))
        windows[2 * i] = jnp.where(marked, marks, even)
        windows[2 * i + 1] = jnp.where(marked, marks, odd)
        return carry

    lax.fori_loop(0, tiles, cut, 0)
    pl.semaphore_wait(barrier, nt - 1 + 3 * has_up.astype(jnp.int32) + 3 * has_down.astype(jnp.int32))

    def window_copy(source, target):
        return pltpu.make_async_remote_copy(
            windows.at[window_of(target)], body.at[body_rows(source + 1, 0, ROWS)], win_send.at[target], win_recv.at[source],
            device_id=(target, z), device_id_type=MESH,
        )

    def send_window(k, carry):
        window_copy(tm, lax.rem(tm + k, nt)).start()
        return carry

    lax.fori_loop(1, nt, send_window, 0)
    body[body_rows(tm + 1, 0, ROWS), :] = windows[mine]

    for load in loads:
        load.wait()
    shift = jnp.where(lax.rem(mine, 2) == 0, SIDE, LANES - SIDE)
    for i in range(3):
        lower, upper = pltpu.roll(pairs[i, 0], shift, 1), pltpu.roll(pairs[i, 1], shift, 1)
        value = jnp.where(lane < shift, lower, upper)
        if i == 0:
            body[:ROWS, :] = value
        params[i, HALO : HALO + ROWS, :] = value

    def params_up():
        return pltpu.make_async_remote_copy(
            params.at[:, pl.ds(HALO, HALO)], params.at[:, pl.ds(HALO + ROWS, HALO)], par_send.at[0], par_recv.at[0],
            device_id=(tm, z - 1), device_id_type=MESH,
        )

    def params_down():
        return pltpu.make_async_remote_copy(
            params.at[:, pl.ds(ROWS, HALO)], params.at[:, pl.ds(0, HALO)], par_send.at[1], par_recv.at[1],
            device_id=(tm, z + 1), device_id_type=MESH,
        )

    def state_up(t, width):
        return pltpu.make_async_remote_copy(
            body.at[body_rows(t, 0, width)], low.at[halo_rows(t, 0, width)], z_send.at[0, t], z_recv.at[0, t],
            device_id=(tm, z - 1), device_id_type=MESH,
        )

    def state_down(t, width):
        return pltpu.make_async_remote_copy(
            body.at[body_rows(t, ROWS - width, width)], high.at[halo_rows(t, HALO - width, width)], z_send.at[1, t], z_recv.at[1, t],
            device_id=(tm, z + 1), device_id_type=MESH,
        )

    @pl.when(has_up)
    def _():
        params_up().start()

    @pl.when(has_down)
    def _():
        params_down().start()

    def forward(width, t, carry):
        @pl.when(t != tm + 1)
        def _():
            window_copy(t - 1, tm).wait_recv()

        @pl.when(has_up)
        def _():
            state_up(t, width).start()

        @pl.when(has_down)
        def _():
            state_down(t, width).start()

        return carry

    def forward_stage(s, carry):
        for first, last, width in widths:
            lax.fori_loop(jnp.maximum(s * SPAN + first, 1), s * SPAN + last, functools.partial(forward, width), 0)
        return carry

    lax.fori_loop(0, nt // SPAN, forward_stage, 0)

    @pl.when(tm != nt - 1)
    def _():
        window_copy(nt - 1, tm).wait_recv()

    def factors(i):
        rows = pl.ds(pl.multiple_of(i * GROUP, GROUP), GROUP)
        row = i * GROUP + lax.broadcasted_iota(jnp.int32, (GROUP, LANES), 0)
        inside = ((row >= HALO) | has_up) & ((row < HALO + ROWS) | has_down)
        kappa = params[1, rows, :]
        for ref, factor in ((fine, 1.0), (coarse, float(STEPS))):
            for k, value in enumerate((1.0 - factor * (4.0 * kappa + 2.0 * ADVECT), factor * (kappa + ADVECT), factor * kappa)):
                value = jnp.where(inside, value, 0.0)
                if ref is fine:
                    fine[k, rows] = jnp.broadcast_to(value[:, None, :], (GROUP, GROUP, LANES))
                else:
                    coarse[k, rows, :] = value
        forcing = jnp.where(inside, params[2, rows, :], 0.0)
        fine[3, rows] = jnp.broadcast_to(forcing[:, None, :], (GROUP, GROUP, LANES))

    def own_factors(i, carry):
        factors(HALO // GROUP + i)
        return carry

    lax.fori_loop(0, ROWS // GROUP, own_factors, 0)

    def body_at(t, r):
        return body[pl.ds(t * ROWS + r, GROUP, stride=ROWS), :]

    def halo_at(ref, t, r):
        return ref[pl.ds(t * HALO + r, GROUP, stride=HALO), :]

    def advance(load, store, amp, first, count):
        for r in range(0, count, BLOCK):
            n = min(BLOCK, count - r)
            u = load(r, n + 2)
            mid = u[1:-1]
            up_left = u[:-2] + pltpu.roll(mid, 1, 2)
            down_right = u[2:] + pltpu.roll(mid, LANES - 1, 2)
            centre, c_up, c_down, forcing = (fine[i, pl.ds(first + r, n)] for i in range(4))
            store(r, n, centre * mid + c_up * up_left + c_down * down_right + amp * forcing)

    def inner_step(source, target, s, k):
        for g in range(PAIR):
            border[s, g, k, 0:2] = source[g, pl.ds(k, 2)]
            border[s, g, k, 2:4] = source[g, pl.ds(ROWS - 2 - k, 2)]

            def load(r, n):
                return source[g, r : r + n]

            def store(r, n, value):
                target[g, r + 1 : r + 1 + n] = value

            advance(load, store, amps[s, g, k], HALO + 1, ROWS - 2)

    def relax_inner(s, carry):
        for g in range(PAIR):
            t = s * SPAN + g * GROUP

            def load_amp(k, carry):
                amps[s, g, k] = jnp.broadcast_to(body_at(t + 1, k)[:, 0:1], (GROUP, LANES))
                return carry

            lax.fori_loop(0, STEPS, load_amp, 0, unroll=2)

            def load_rows(i, carry):
                for r in range(GROUP):
                    inner[g, i * GROUP + r] = body_at(t, i * GROUP + r)
                return carry

            lax.fori_loop(0, ROWS // GROUP, load_rows, 0)

        def two_steps(k, carry):
            inner_step(inner, inner_next, s, 2 * k)
            inner_step(inner_next, inner, s, 2 * k + 1)
            return carry

        lax.fori_loop(0, STEPS // 2, two_steps, 0)
        for g in range(PAIR):
            core[s, g] = inner[g, STEPS : STEPS + CORE]
        return carry

    lax.fori_loop(0, nt // SPAN, relax_inner, 0)

    @pl.when(has_down)
    def _():
        params_up().wait_recv()

    @pl.when(has_up)
    def _():
        params_down().wait_recv()

    high[:HALO, :] = params[0, :HALO, :]
    low[:HALO, :] = params[0, HALO + ROWS :, :]

    def halo_factors(i, carry):
        factors(jnp.where(i < HALO // GROUP, i, i + ROWS // GROUP))
        return carry

    lax.fori_loop(0, 2 * HALO // GROUP, halo_factors, 0)

    def arrive(width, t, carry):
        @pl.when(has_down)
        def _():
            state_up(t, width).wait_recv()

        @pl.when(has_up)
        def _():
            state_down(t, width).wait_recv()

        return carry

    def arrivals(s):
        for first, last, width in widths:
            lax.fori_loop(s * SPAN + max(first, 1), s * SPAN + last, functools.partial(arrive, width), 0)

        @pl.when(s < nt // SPAN - 1)
        def _():
            arrive(HALO, (s + 1) * SPAN, 0)

    def outer_step(source, target, s, k):
        for g in range(PAIR):
            for side in range(2):
                def load(r, n):
                    if side == 0 and r + n > HALO:
                        return jnp.concatenate([source[g, 0, r:HALO], border[s, g, k, 0 : r + n - HALO]], axis=0)
                    if side == 1 and r < 2:
                        return jnp.concatenate([border[s, g, k, 2 + r : 4], source[g, 1, 0 : r + n - 2]], axis=0)
                    first = r - 2 * side
                    return source[g, side, first : first + n]

                def store(r, n, value):
                    target[g, side, r : r + n] = value

                advance(load, store, amps[s, g, k], k + 1 if side == 0 else HALO + ROWS - 1 - k, HALO)

    def relax(s):
        arrivals(s)
        for g in range(PAIR):
            t = s * SPAN + g * GROUP

            def load_rows(i, carry):
                for r in range(GROUP):
                    outer[g, 0, i * GROUP + r] = halo_at(high, t, i * GROUP + r)
                    outer[g, 1, i * GROUP + r] = halo_at(low, t, i * GROUP + r)
                return carry

            lax.fori_loop(0, HALO // GROUP, load_rows, 0)

        def two_steps(k, carry):
            outer_step(outer, outer_next, s, 2 * k)
            outer_step(outer_next, outer, s, 2 * k + 1)
            return carry

        lax.fori_loop(0, STEPS // 2, two_steps, 0)

        for g in range(PAIR):
            t = s * SPAN + g * GROUP

            def put(row, value):
                residual[s * PAIR + g, pl.ds(pl.multiple_of((row - STEPS) * GROUP, GROUP), GROUP), :] = value

            def finish_halo(i, carry):
                for r in range(GROUP):
                    row = i * GROUP + r
                    put(STEPS + row, outer[g, 0, row] - halo_at(high, t + 1, STEPS + row))
                    put(HALO + ROWS + row, outer[g, 1, STEPS + row] - halo_at(low, t + 1, row))
                return carry

            lax.fori_loop(0, (HALO - STEPS) // GROUP, finish_halo, 0)
            for r in range(STEPS):
                put(HALO + r, outer[g, 0, HALO - STEPS + r] - body_at(t + 1, r))
                put(HALO + ROWS - STEPS + r, outer[g, 1, r] - body_at(t + 1, ROWS - STEPS + r))

            def finish_core(i, carry):
                for r in range(GROUP):
                    row = i * GROUP + r
                    put(HALO + STEPS + row, core[s, g, row] - body_at(t + 1, STEPS + row))
                return carry

            lax.fori_loop(0, CORE // GROUP, finish_core, 0)

    def back_copy(source, target):
        return pltpu.make_async_remote_copy(
            packed.at[target], arrived.at[window_of(source)], back_send.at[target], back_recv.at[source],
            device_id=(target, z), device_id_type=MESH,
        )

    half = ROWS // 2
    lane_half = lanes_of((half, LANES))

    def sweep(group, e):
        centre, c_up, c_down = ([coarse[i, pl.ds(STEPS + b, 8, stride=8), :] for b in range(8)] for i in range(3))

        def step(place, e):
            t = group * GROUP + place
            above = [pltpu.roll(e[7], 1, 0)] + e[:7]
            below = e[1:] + [pltpu.roll(e[0], 7, 0)]
            after = []
            for b in range(8):
                up_left = above[b] + pltpu.roll(e[b], 1, 1)
                down_right = below[b] + pltpu.roll(e[b], LANES - 1, 1)
                add = residual[group, pl.ds(b * GROUP + place, 8, stride=8 * GROUP), :]
                after.append(centre[b] * e[b] + c_up[b] * up_left + c_down[b] * down_right + add)
            for b in range(8):
                error[t, pl.ds(b, 8, stride=8), :] = after[b]
            return after

        def pack(place):
            t = group * GROUP + place
            top, bottom = error[t, SPAN : SPAN + half, :], error[t, SPAN + half : SPAN + ROWS, :]
            packed[t] = jnp.where(lane_half < OWN, pltpu.roll(top, LANES - SIDE, 1), pltpu.roll(bottom, SIDE, 1))

        def pack_and_step(place, e):
            pack(place - 1)
            return step(place, e)

        e = lax.fori_loop(1, GROUP, pack_and_step, step(0, e))
        pack(GROUP - 1)

        def give(t, carry):
            @pl.when(t != tm)
            def _():
                back_copy(tm, t).start()

            return carry

        lax.fori_loop(group * GROUP, (group + 1) * GROUP, give, 0)
        return e

    edge_rows = {-1: (pl.ds(SPAN, SPAN), pl.ds(SPAN + ROWS, SPAN)), 1: (pl.ds(ROWS, SPAN), pl.ds(0, SPAN)), 0: (pl.ds(SPAN, ROWS), pl.ds(SPAN, ROWS))}

    def edge_copies(s):
        for dz in (-1, 0, 1):
            for slot, target in ((2, before), (1, tm), (0, after)):
                if dz == 0 and slot == 1:
                    continue
                rows_here, rows_there = edge_rows[dz]
                copy = pltpu.make_async_remote_copy(
                    error.at[(s + 1) * SPAN - 1, rows_here], edges.at[s, slot, rows_there], edge_send.at[s, slot, dz + 1], edge_recv.at[s, slot, dz + 1],
                    device_id=(target, z + dz), device_id_type=MESH,
                )
                yield dz, copy

    def when_dz(dz, send, do):
        if dz == 0:
            do()
        else:
            up = (dz == -1) == send
            pl.when(has_up if up else has_down)(do)

    stages = nt // SPAN
    lane_trim = lanes_of((TRIM, LANES))
    row_trim = lax.broadcasted_iota(jnp.int32, (TRIM, LANES), 0)
    centre = (row_trim >= SPAN) & (row_trim < SPAN + ROWS)

    groups = SPAN // GROUP
    starts[...] = jnp.zeros((TRIM, LANES), jnp.float32)

    def stage(s, carry):
        relax(s)

        @pl.when(s > 0)
        def _():
            for dz, copy in edge_copies(s - 1):
                when_dz(dz, False, copy.wait_recv)
            left = pltpu.roll(edges[s - 1, 0], OWN, 1)
            right = pltpu.roll(edges[s - 1, 2], OWN, 1)
            own = jnp.where(centre, error[s * SPAN - 1], edges[s - 1, 1])
            starts[...] = jnp.where(lane_trim < SIDE, left, jnp.where(lane_trim >= LANES - SIDE, right, own))

        e = [starts[pl.ds(b, 8, stride=8), :] for b in range(8)]
        lax.fori_loop(s * groups, (s + 1) * groups, sweep, e)

        @pl.when(s < stages - 1)
        def _():
            for dz, copy in edge_copies(s):
                when_dz(dz, True, copy.start)

        return carry

    lax.fori_loop(0, stages, stage, 0)

    def sent(k, carry):
        window_copy(tm, lax.rem(tm + k, nt)).wait_send()
        return carry

    lax.fori_loop(1, nt, sent, 0)

    def drain(copy):
        def drain_stage(s, carry):
            for first, last, width in widths:
                lax.fori_loop(
                    jnp.maximum(s * SPAN + first, 1), s * SPAN + last, lambda t, carry: (copy(t, width).wait_send(), carry)[1], 0
                )
            return carry

        lax.fori_loop(0, nt // SPAN, drain_stage, 0)

    @pl.when(has_up)
    def _():
        params_up().wait_send()
        drain(state_up)

    @pl.when(has_down)
    def _():
        params_down().wait_send()
        drain(state_down)

    for s in range(stages - 1):
        for dz, copy in edge_copies(s):
            when_dz(dz, True, copy.wait_send)

    def collect(k, carry):
        back_copy(lax.rem(tm + k, nt), tm).wait_recv()
        back_copy(tm, lax.rem(tm + k, nt)).wait_send()
        return carry

    lax.fori_loop(1, nt, collect, 0)

    def join(i, carry):
        first, second = arrived[2 * i], arrived[2 * i + 1]
        columns = pl.ds(pl.multiple_of(i * LANES, LANES), LANES)
        top = jnp.where(lane_half < OWN, first, pltpu.roll(second, OWN, 1))
        bottom = jnp.where(lane_half < OWN, pltpu.roll(first, OWN, 1), second)
        out_ref[0, :half, columns] = guess[:half, columns] + top
        out_ref[0, half:, columns] = guess[half:, columns] + bottom
        return carry

    arrived[mine] = packed[tm]
    lax.fori_loop(0, tiles, join, 0, unroll=4)


def per_device(initial_state, guesses, diffusivity, forcing_field, amplitudes):
    nt, nz = lax.axis_size("tm"), lax.axis_size("space")
    rows, cols = initial_state.shape
    stages = nt // SPAN
    dma = pltpu.SemaphoreType.DMA
    vmem = functools.partial(pltpu.VMEM, dtype=jnp.float32)
    hbm = pl.BlockSpec(memory_space=pl.ANY)
    return pl.pallas_call(
        functools.partial(kernel, nt, nz),
        out_shape=jax.ShapeDtypeStruct((1, rows, cols), jnp.float32),
        in_specs=[hbm] * 5,
        out_specs=pl.BlockSpec(memory_space=pltpu.VMEM),
        scratch_shapes=[
            pltpu.SMEM((STEPS,), jnp.float32),
            vmem((rows, cols)),
            vmem((3, 2, rows, LANES)),
            vmem((nt, rows, LANES)),
            vmem((3, TALL, LANES)),
            vmem(((nt + 1) * ROWS, LANES)),
            vmem(((nt + 1) * HALO, LANES)),
            vmem(((nt + 1) * HALO, LANES)),
            vmem((3, TALL, LANES)),
            vmem((4, TALL, GROUP, LANES)),
            vmem((nt // SPAN, PAIR, STEPS, GROUP, LANES)),
            vmem((PAIR, ROWS, GROUP, LANES)),
            vmem((PAIR, ROWS, GROUP, LANES)),
            vmem((nt // SPAN, PAIR, STEPS, 4, GROUP, LANES)),
            vmem((nt // SPAN, PAIR, CORE, GROUP, LANES)),
            vmem((PAIR, 2, HALO, GROUP, LANES)),
            vmem((PAIR, 2, HALO, GROUP, LANES)),
            vmem((nt // GROUP, TRIM * GROUP, LANES)),
            vmem((nt, TRIM, LANES)),
            vmem((stages - 1, 3, TRIM, LANES)),
            vmem((TRIM, LANES)),
            vmem((nt, rows // 2, LANES)),
            vmem((nt, rows // 2, LANES)),
            dma, dma, dma((3, 2)), dma((nt,)), dma((nt,)), dma((2,)), dma((2,)), dma((2, nt + 1)), dma((2, nt + 1)),
            dma((stages - 1, 3, 3)), dma((stages - 1, 3, 3)), dma((nt,)), dma((nt,)),
        ],
        compiler_params=pltpu.CompilerParams(collective_id=0, has_side_effects=True, vmem_limit_bytes=VMEM_LIMIT),
    )(initial_state, guesses, diffusivity, forcing_field, amplitudes)


def solution(mesh):
    placed = (P("space", None), P("tm", "space", None), P("space", None), P("space", None), P("tm"))
    return jax.shard_map(
        per_device, mesh=mesh, in_specs=placed, out_specs=P("tm", "space", None), check_vma=False
    )
```

```python
import functools

import jax
import jax.numpy as jnp
from jax import lax
from jax.experimental import pallas as pl
from jax.experimental.pallas import tpu as pltpu
from jax.sharding import PartitionSpec as P

MESH = pl.DeviceIdType.MESH
ADVECT = 0.01
LANES = 128
STEPS = 8
SPAN = 16
ROWS = 32
HALO = STEPS + SPAN
TALL = ROWS + 2 * HALO
TRIM = TALL - 2 * STEPS
GROUP = 8
PAIR = SPAN // GROUP
CORE = ROWS - 2 * STEPS
BLOCK = 8
ACROSS = 8
SIDE = 32
OWN = LANES - 2 * SIDE
VMEM_LIMIT = 536 * 2**20 // 10


def width_of(place):
    return (STEPS + SPAN - 1 - place + 7) // 8 * 8


def spans():
    found = []
    for place in range(SPAN):
        if found and found[-1][2] == width_of(place):
            found[-1][1] = place + 1
        else:
            found.append([place, place + 1, width_of(place)])
    return found


def window_of(device):
    turn = lax.rem(lax.div(device, ACROSS), 2)
    place = lax.rem(device, ACROSS)
    return device - place + jnp.where(turn == 1, ACROSS - 1 - place, place)


def lanes_of(shape):
    return lax.broadcasted_iota(jnp.int32, shape, 1)


def kernel(
    nt, nz, initial_hbm, guess_hbm, kappa_hbm, forcing_hbm, amp_hbm, out_ref,
    amp_ref, guess, pairs, windows, params, body, high, low, coarse, fine, amps, inner, inner_next, border, core, outer, outer_next, residual, error, edges, starts, packed, arrived,
    amp_sem, load_sem, pair_sem, win_send, win_recv, par_send, par_recv, z_send, z_recv, edge_send, edge_recv, back_send, back_recv,
):
    tm, z = lax.axis_index("tm"), lax.axis_index("space")
    tiles = guess.shape[1] // LANES
    widths = spans()
    has_up, has_down = z > 0, z < nz - 1
    mine = window_of(tm)
    before, after = window_of(lax.rem(mine + nt - 1, nt)), window_of(lax.rem(mine + 1, nt))

    barrier = pltpu.get_barrier_semaphore()

    def greet(t, where):
        pl.semaphore_signal(barrier, inc=1, device_id=(t, where), device_id_type=MESH)

    def greet_plane(k, carry):
        greet(lax.rem(tm + k, nt), z)
        return carry

    lax.fori_loop(1, nt, greet_plane, 0)

    @pl.when(has_up)
    def _():
        for t in (tm, before, after):
            greet(t, z - 1)

    @pl.when(has_down)
    def _():
        for t in (tm, before, after):
            greet(t, z + 1)

    load_guess = pltpu.make_async_copy(guess_hbm.at[0], guess, load_sem)
    load_guess.start()
    load_amps = pltpu.make_async_copy(amp_hbm, amp_ref, amp_sem)
    load_amps.start()
    first = lax.rem(lax.div(mine + nt - 1, 2), tiles)
    second = lax.rem(first + 1, tiles)
    loads = []
    for i, ref in enumerate((initial_hbm, kappa_hbm, forcing_hbm)):
        for k, tile in enumerate((first, second)):
            columns = pl.ds(pl.multiple_of(tile * LANES, LANES), LANES)
            loads.append(pltpu.make_async_copy(ref.at[:, columns], pairs.at[i, k], pair_sem.at[i, k]))
    for load in loads:
        load.start()

    def body_rows(t, first, count):
        return pl.ds(pl.multiple_of(t * ROWS + first, 8), count)

    def halo_rows(t, first, count):
        return pl.ds(pl.multiple_of(t * HALO + first, 8), count)

    def clear(ref, t, carry):
        ref[halo_rows(t, 0, HALO), :] = jnp.zeros((HALO, LANES), jnp.float32)
        return carry

    @pl.when(jnp.logical_not(has_up))
    def _():
        params[:, :HALO, :] = jnp.zeros((3, HALO, LANES), jnp.float32)
        lax.fori_loop(0, nt + 1, functools.partial(clear, high), 0)

    @pl.when(jnp.logical_not(has_down))
    def _():
        params[:, HALO + ROWS :, :] = jnp.zeros((3, HALO, LANES), jnp.float32)
        lax.fori_loop(0, nt + 1, functools.partial(clear, low), 0)

    @pl.when(jnp.logical_not(has_up))
    def _():
        edges[:, :, :SPAN, :] = jnp.zeros((nt // SPAN - 1, 3, SPAN, LANES), jnp.float32)

    @pl.when(jnp.logical_not(has_down))
    def _():
        edges[:, :, SPAN + ROWS :, :] = jnp.zeros((nt // SPAN - 1, 3, SPAN, LANES), jnp.float32)

    row_index = lax.broadcasted_iota(jnp.int32, (ROWS, LANES), 0)
    lane = lanes_of((ROWS, LANES))
    marks = jnp.zeros((ROWS, LANES), jnp.float32)
    load_amps.wait()
    for k in range(STEPS):
        marks = jnp.where(row_index == k, amp_ref[k], marks)
    marked = (lane == 0) & (row_index < STEPS)

    load_guess.wait()

    def tile_of(i):
        return guess[:, pl.ds(pl.multiple_of(i * LANES, LANES), LANES)]

    def cut(i, carry):
        low, mid, high = (tile_of(lax.rem(i + d, tiles)) for d in (tiles - 1, 0, 1))
        even = jnp.where(lane < SIDE, pltpu.roll(low, SIDE, 1), pltpu.roll(mid, SIDE, 1))
        odd = jnp.where(lane < LANES - SIDE, pltpu.roll(mid, LANES - SIDE, 1), pltpu.roll(high, LANES - SIDE, 1))
        windows[2 * i] = jnp.where(marked, marks, even)
        windows[2 * i + 1] = jnp.where(marked, marks, odd)
        return carry

    lax.fori_loop(0, tiles, cut, 0)
    pl.semaphore_wait(barrier, nt - 1 + 3 * has_up.astype(jnp.int32) + 3 * has_down.astype(jnp.int32))

    def window_copy(source, target):
        return pltpu.make_async_remote_copy(
            windows.at[window_of(target)], body.at[body_rows(source + 1, 0, ROWS)], win_send.at[target], win_recv.at[source],
            device_id=(target, z), device_id_type=MESH,
        )

    def send_window(k, carry):
        window_copy(tm, lax.rem(tm + k, nt)).start()
        return carry

    lax.fori_loop(1, nt, send_window, 0)
    body[body_rows(tm + 1, 0, ROWS), :] = windows[mine]

    for load in loads:
        load.wait()
    shift = jnp.where(lax.rem(mine, 2) == 0, SIDE, LANES - SIDE)
    for i in range(3):
        lower, upper = pltpu.roll(pairs[i, 0], shift, 1), pltpu.roll(pairs[i, 1], shift, 1)
        value = jnp.where(lane < shift, lower, upper)
        if i == 0:
            body[:ROWS, :] = value
        params[i, HALO : HALO + ROWS, :] = value

    def params_up():
        return pltpu.make_async_remote_copy(
            params.at[:, pl.ds(HALO, HALO)], params.at[:, pl.ds(HALO + ROWS, HALO)], par_send.at[0], par_recv.at[0],
            device_id=(tm, z - 1), device_id_type=MESH,
        )

    def params_down():
        return pltpu.make_async_remote_copy(
            params.at[:, pl.ds(ROWS, HALO)], params.at[:, pl.ds(0, HALO)], par_send.at[1], par_recv.at[1],
            device_id=(tm, z + 1), device_id_type=MESH,
        )

    def state_up(t, width):
        return pltpu.make_async_remote_copy(
            body.at[body_rows(t, 0, width)], low.at[halo_rows(t, 0, width)], z_send.at[0, t], z_recv.at[0, t],
            device_id=(tm, z - 1), device_id_type=MESH,
        )

    def state_down(t, width):
        return pltpu.make_async_remote_copy(
            body.at[body_rows(t, ROWS - width, width)], high.at[halo_rows(t, HALO - width, width)], z_send.at[1, t], z_recv.at[1, t],
            device_id=(tm, z + 1), device_id_type=MESH,
        )

    @pl.when(has_up)
    def _():
        params_up().start()

    @pl.when(has_down)
    def _():
        params_down().start()

    def forward(width, t, carry):
        @pl.when(t != tm + 1)
        def _():
            window_copy(t - 1, tm).wait_recv()

        @pl.when(has_up)
        def _():
            state_up(t, width).start()

        @pl.when(has_down)
        def _():
            state_down(t, width).start()

        return carry

    def forward_stage(s, carry):
        for first, last, width in widths:
            lax.fori_loop(jnp.maximum(s * SPAN + first, 1), s * SPAN + last, functools.partial(forward, width), 0)
        return carry

    lax.fori_loop(0, nt // SPAN, forward_stage, 0)

    @pl.when(tm != nt - 1)
    def _():
        window_copy(nt - 1, tm).wait_recv()

    def factors(i):
        rows = pl.ds(pl.multiple_of(i * GROUP, GROUP), GROUP)
        row = i * GROUP + lax.broadcasted_iota(jnp.int32, (GROUP, LANES), 0)
        inside = ((row >= HALO) | has_up) & ((row < HALO + ROWS) | has_down)
        kappa = params[1, rows, :]
        for ref, factor in ((fine, 1.0), (coarse, float(STEPS))):
            for k, value in enumerate((1.0 - factor * (4.0 * kappa + 2.0 * ADVECT), factor * (kappa + ADVECT), factor * kappa)):
                value = jnp.where(inside, value, 0.0)
                if ref is fine:
                    fine[k, rows] = jnp.broadcast_to(value[:, None, :], (GROUP, GROUP, LANES))
                else:
                    coarse[k, rows, :] = value
        forcing = jnp.where(inside, params[2, rows, :], 0.0)
        fine[3, rows] = jnp.broadcast_to(forcing[:, None, :], (GROUP, GROUP, LANES))

    def own_factors(i, carry):
        factors(HALO // GROUP + i)
        return carry

    lax.fori_loop(0, ROWS // GROUP, own_factors, 0)

    def body_at(t, r):
        return body[pl.ds(t * ROWS + r, GROUP, stride=ROWS), :]

    def halo_at(ref, t, r):
        return ref[pl.ds(t * HALO + r, GROUP, stride=HALO), :]

    def advance(load, store, amp, first, begin, end):
        for r in range(begin, end, BLOCK):
            n = min(BLOCK, end - r)
            u = load(r, n + 2)
            mid = u[1:-1]
            up_left = u[:-2] + pltpu.roll(mid, 1, 2)
            down_right = u[2:] + pltpu.roll(mid, LANES - 1, 2)
            centre, c_up, c_down, forcing = (fine[i, pl.ds(first + r, n)] for i in range(4))
            store(r, n, centre * mid + c_up * up_left + c_down * down_right + amp * forcing)

    def inner_step(source, target, s, k):
        for g in range(PAIR):
            border[s, g, k, 0:2] = source[g, pl.ds(k, 2)]
            border[s, g, k, 2:4] = source[g, pl.ds(ROWS - 2 - k, 2)]

            def load(r, n):
                return source[g, r : r + n]

            def store(r, n, value):
                target[g, r + 1 : r + 1 + n] = value

            advance(load, store, amps[s, g, k], HALO + 1, 0, ROWS - 2)

    def relax_inner(s, carry):
        for g in range(PAIR):
            t = s * SPAN + g * GROUP

            def load_amp(k, carry):
                amps[s, g, k] = jnp.broadcast_to(body_at(t + 1, k)[:, 0:1], (GROUP, LANES))
                return carry

            lax.fori_loop(0, STEPS, load_amp, 0, unroll=2)

            def load_rows(i, carry):
                for r in range(GROUP):
                    inner[g, i * GROUP + r] = body_at(t, i * GROUP + r)
                return carry

            lax.fori_loop(0, ROWS // GROUP, load_rows, 0)

        def two_steps(k, carry):
            inner_step(inner, inner_next, s, 2 * k)
            inner_step(inner_next, inner, s, 2 * k + 1)
            return carry

        lax.fori_loop(0, STEPS // 2, two_steps, 0)
        for g in range(PAIR):
            core[s, g] = inner[g, STEPS : STEPS + CORE]
        return carry

    lax.fori_loop(0, nt // SPAN, relax_inner, 0)

    @pl.when(has_down)
    def _():
        params_up().wait_recv()

    @pl.when(has_up)
    def _():
        params_down().wait_recv()

    high[:HALO, :] = params[0, :HALO, :]
    low[:HALO, :] = params[0, HALO + ROWS :, :]

    def halo_factors(i, carry):
        factors(jnp.where(i < HALO // GROUP, i, i + ROWS // GROUP))
        return carry

    lax.fori_loop(0, 2 * HALO // GROUP, halo_factors, 0)

    def arrive(width, t, carry):
        @pl.when(has_down)
        def _():
            state_up(t, width).wait_recv()

        @pl.when(has_up)
        def _():
            state_down(t, width).wait_recv()

        return carry

    def arrivals(s):
        for first, last, width in widths:
            lax.fori_loop(s * SPAN + max(first, 1), s * SPAN + last, functools.partial(arrive, width), 0)

        @pl.when(s < nt // SPAN - 1)
        def _():
            arrive(HALO, (s + 1) * SPAN, 0)

    def outer_step(source, target, s, k):
        for g in range(PAIR):
            for side in range(2):
                def load(r, n):
                    if side == 0 and r + n > HALO:
                        return jnp.concatenate([source[g, 0, r:HALO], border[s, g, k, 0 : r + n - HALO]], axis=0)
                    if side == 1 and r < 2:
                        return jnp.concatenate([border[s, g, k, 2 + r : 4], source[g, 1, 0 : r + n - 2]], axis=0)
                    first = r - 2 * side
                    return source[g, side, first : first + n]

                def store(r, n, value):
                    target[g, side, r : r + n] = value

                skip = g * GROUP
                if side == 0:
                    advance(load, store, amps[s, g, k], k + 1, skip, HALO)
                else:
                    advance(load, store, amps[s, g, k], HALO + ROWS - 1 - k, 0, HALO - skip)

    def relax(s):
        arrivals(s)
        for g in range(PAIR):
            t = s * SPAN + g * GROUP

            def load_rows(i, carry):
                for r in range(GROUP):
                    outer[g, 0, i * GROUP + r] = halo_at(high, t, i * GROUP + r)
                    outer[g, 1, i * GROUP + r] = halo_at(low, t, i * GROUP + r)
                return carry

            lax.fori_loop(0, HALO // GROUP, load_rows, 0)

        def two_steps(k, carry):
            outer_step(outer, outer_next, s, 2 * k)
            outer_step(outer_next, outer, s, 2 * k + 1)
            return carry

        lax.fori_loop(0, STEPS // 2, two_steps, 0)

        for g in range(PAIR):
            t = s * SPAN + g * GROUP

            def put(row, value):
                residual[s * PAIR + g, pl.ds(pl.multiple_of((row - STEPS) * GROUP, GROUP), GROUP), :] = value

            def finish_halo(i, carry):
                for r in range(GROUP):
                    row = i * GROUP + r
                    put(STEPS + row, outer[g, 0, row] - halo_at(high, t + 1, STEPS + row))
                    put(HALO + ROWS + row, outer[g, 1, STEPS + row] - halo_at(low, t + 1, row))
                return carry

            lax.fori_loop(0, (HALO - STEPS) // GROUP, finish_halo, 0)
            for r in range(STEPS):
                put(HALO + r, outer[g, 0, HALO - STEPS + r] - body_at(t + 1, r))
                put(HALO + ROWS - STEPS + r, outer[g, 1, r] - body_at(t + 1, ROWS - STEPS + r))

            def finish_core(i, carry):
                for r in range(GROUP):
                    row = i * GROUP + r
                    put(HALO + STEPS + row, core[s, g, row] - body_at(t + 1, STEPS + row))
                return carry

            lax.fori_loop(0, CORE // GROUP, finish_core, 0)

    def back_copy(source, target):
        return pltpu.make_async_remote_copy(
            packed.at[target], arrived.at[window_of(source)], back_send.at[target], back_recv.at[source],
            device_id=(target, z), device_id_type=MESH,
        )

    half = ROWS // 2
    lane_half = lanes_of((half, LANES))

    def sweep(group, e):
        centre, c_up, c_down = ([coarse[i, pl.ds(STEPS + b, 8, stride=8), :] for b in range(8)] for i in range(3))

        def step(place, e):
            t = group * GROUP + place
            above = [pltpu.roll(e[7], 1, 0)] + e[:7]
            below = e[1:] + [pltpu.roll(e[0], 7, 0)]
            after = []
            for b in range(8):
                up_left = above[b] + pltpu.roll(e[b], 1, 1)
                down_right = below[b] + pltpu.roll(e[b], LANES - 1, 1)
                add = residual[group, pl.ds(b * GROUP + place, 8, stride=8 * GROUP), :]
                after.append(centre[b] * e[b] + c_up[b] * up_left + c_down[b] * down_right + add)
            for b in range(8):
                error[t, pl.ds(b, 8, stride=8), :] = after[b]
            return after

        def pack(place):
            t = group * GROUP + place
            top, bottom = error[t, SPAN : SPAN + half, :], error[t, SPAN + half : SPAN + ROWS, :]
            packed[t] = jnp.where(lane_half < OWN, pltpu.roll(top, LANES - SIDE, 1), pltpu.roll(bottom, SIDE, 1))

        def pack_and_step(place, e):
            pack(place - 1)
            return step(place, e)

        e = lax.fori_loop(1, GROUP, pack_and_step, step(0, e), unroll=7)

        @pl.when((lax.rem(group, PAIR) == PAIR - 1) & (group < nt // GROUP - 1))
        def _():
            for dz, copy in edge_copies(lax.div(group, PAIR)):
                when_dz(dz, True, copy.start)

        pack(GROUP - 1)

        def give(t, carry):
            @pl.when(t != tm)
            def _():
                back_copy(tm, t).start()

            return carry

        lax.fori_loop(group * GROUP, (group + 1) * GROUP, give, 0)
        return e

    edge_rows = {-1: (pl.ds(SPAN, SPAN), pl.ds(SPAN + ROWS, SPAN)), 1: (pl.ds(ROWS, SPAN), pl.ds(0, SPAN)), 0: (pl.ds(SPAN, ROWS), pl.ds(SPAN, ROWS))}

    def edge_copies(s):
        for dz in (-1, 0, 1):
            for slot, target in ((2, before), (1, tm), (0, after)):
                if dz == 0 and slot == 1:
                    continue
                rows_here, rows_there = edge_rows[dz]
                copy = pltpu.make_async_remote_copy(
                    error.at[(s + 1) * SPAN - 1, rows_here], edges.at[s, slot, rows_there], edge_send.at[s, slot, dz + 1], edge_recv.at[s, slot, dz + 1],
                    device_id=(target, z + dz), device_id_type=MESH,
                )
                yield dz, copy

    def when_dz(dz, send, do):
        if dz == 0:
            do()
        else:
            up = (dz == -1) == send
            pl.when(has_up if up else has_down)(do)

    stages = nt // SPAN
    lane_trim = lanes_of((TRIM, LANES))
    row_trim = lax.broadcasted_iota(jnp.int32, (TRIM, LANES), 0)
    centre = (row_trim >= SPAN) & (row_trim < SPAN + ROWS)

    groups = SPAN // GROUP
    starts[...] = jnp.zeros((TRIM, LANES), jnp.float32)

    def stage(s, carry):
        relax(s)

        @pl.when(s > 0)
        def _():
            for dz, copy in edge_copies(s - 1):
                when_dz(dz, False, copy.wait_recv)
            left = pltpu.roll(edges[s - 1, 0], OWN, 1)
            right = pltpu.roll(edges[s - 1, 2], OWN, 1)
            own = jnp.where(centre, error[s * SPAN - 1], edges[s - 1, 1])
            starts[...] = jnp.where(lane_trim < SIDE, left, jnp.where(lane_trim >= LANES - SIDE, right, own))

        e = [starts[pl.ds(b, 8, stride=8), :] for b in range(8)]
        lax.fori_loop(s * groups, (s + 1) * groups, sweep, e)

        return carry

    lax.fori_loop(0, stages, stage, 0)

    def sent(k, carry):
        window_copy(tm, lax.rem(tm + k, nt)).wait_send()
        return carry

    lax.fori_loop(1, nt, sent, 0)

    def drain(copy):
        def drain_stage(s, carry):
            for first, last, width in widths:
                lax.fori_loop(
                    jnp.maximum(s * SPAN + first, 1), s * SPAN + last, lambda t, carry: (copy(t, width).wait_send(), carry)[1], 0
                )
            return carry

        lax.fori_loop(0, nt // SPAN, drain_stage, 0)

    @pl.when(has_up)
    def _():
        params_up().wait_send()
        drain(state_up)

    @pl.when(has_down)
    def _():
        params_down().wait_send()
        drain(state_down)

    for s in range(stages - 1):
        for dz, copy in edge_copies(s):
            when_dz(dz, True, copy.wait_send)

    def collect(k, carry):
        back_copy(lax.rem(tm + k, nt), tm).wait_recv()
        back_copy(tm, lax.rem(tm + k, nt)).wait_send()
        return carry

    lax.fori_loop(1, nt, collect, 0)

    def join(i, carry):
        first, second = arrived[2 * i], arrived[2 * i + 1]
        columns = pl.ds(pl.multiple_of(i * LANES, LANES), LANES)
        top = jnp.where(lane_half < OWN, first, pltpu.roll(second, OWN, 1))
        bottom = jnp.where(lane_half < OWN, pltpu.roll(first, OWN, 1), second)
        out_ref[0, :half, columns] = guess[:half, columns] + top
        out_ref[0, half:, columns] = guess[half:, columns] + bottom
        return carry

    arrived[mine] = packed[tm]
    lax.fori_loop(0, tiles, join, 0, unroll=8)


def per_device(initial_state, guesses, diffusivity, forcing_field, amplitudes):
    nt, nz = lax.axis_size("tm"), lax.axis_size("space")
    rows, cols = initial_state.shape
    stages = nt // SPAN
    dma = pltpu.SemaphoreType.DMA
    vmem = functools.partial(pltpu.VMEM, dtype=jnp.float32)
    hbm = pl.BlockSpec(memory_space=pl.ANY)
    return pl.pallas_call(
        functools.partial(kernel, nt, nz),
        out_shape=jax.ShapeDtypeStruct((1, rows, cols), jnp.float32),
        in_specs=[hbm] * 5,
        out_specs=pl.BlockSpec(memory_space=pltpu.VMEM),
        scratch_shapes=[
            pltpu.SMEM((STEPS,), jnp.float32),
            vmem((rows, cols)),
            vmem((3, 2, rows, LANES)),
            vmem((nt, rows, LANES)),
            vmem((3, TALL, LANES)),
            vmem(((nt + 1) * ROWS, LANES)),
            vmem(((nt + 1) * HALO, LANES)),
            vmem(((nt + 1) * HALO, LANES)),
            vmem((3, TALL, LANES)),
            vmem((4, TALL, GROUP, LANES)),
            vmem((nt // SPAN, PAIR, STEPS, GROUP, LANES)),
            vmem((PAIR, ROWS, GROUP, LANES)),
            vmem((PAIR, ROWS, GROUP, LANES)),
            vmem((nt // SPAN, PAIR, STEPS, 4, GROUP, LANES)),
            vmem((nt // SPAN, PAIR, CORE, GROUP, LANES)),
            vmem((PAIR, 2, HALO, GROUP, LANES)),
            vmem((PAIR, 2, HALO, GROUP, LANES)),
            vmem((nt // GROUP, TRIM * GROUP, LANES)),
            vmem((nt, TRIM, LANES)),
            vmem((stages - 1, 3, TRIM, LANES)),
            vmem((TRIM, LANES)),
            vmem((nt, rows // 2, LANES)),
            vmem((nt, rows // 2, LANES)),
            dma, dma, dma((3, 2)), dma((nt,)), dma((nt,)), dma((2,)), dma((2,)), dma((2, nt + 1)), dma((2, nt + 1)),
            dma((stages - 1, 3, 3)), dma((stages - 1, 3, 3)), dma((nt,)), dma((nt,)),
        ],
        compiler_params=pltpu.CompilerParams(collective_id=0, has_side_effects=True, vmem_limit_bytes=VMEM_LIMIT),
    )(initial_state, guesses, diffusivity, forcing_field, amplitudes)


def solution(mesh):
    placed = (P("space", None), P("tm", "space", None), P("space", None), P("space", None), P("tm"))
    return jax.shard_map(
        per_device, mesh=mesh, in_specs=placed, out_specs=P("tm", "space", None), check_vma=False
    )
```

```python
import functools

import jax
import jax.numpy as jnp
from jax import lax
from jax.experimental import pallas as pl
from jax.experimental.pallas import tpu as pltpu
from jax.sharding import PartitionSpec as P

MESH = pl.DeviceIdType.MESH
ADVECT = 0.01
LANES = 128
STEPS = 8
SPAN = 16
ROWS = 32
HALO = STEPS + SPAN
TALL = ROWS + 2 * HALO
TRIM = TALL - 2 * STEPS
GROUP = 8
PAIR = SPAN // GROUP
CORE = ROWS - 2 * STEPS
BLOCK = 8
ACROSS = 8
SIDE = 32
OWN = LANES - 2 * SIDE
VMEM_LIMIT = 536 * 2**20 // 10


def width_of(place):
    return (STEPS + SPAN - 1 - place + 7) // 8 * 8


def spans():
    found = []
    for place in range(SPAN):
        if found and found[-1][2] == width_of(place):
            found[-1][1] = place + 1
        else:
            found.append([place, place + 1, width_of(place)])
    return found


def window_of(device):
    turn = lax.rem(lax.div(device, ACROSS), 2)
    place = lax.rem(device, ACROSS)
    return device - place + jnp.where(turn == 1, ACROSS - 1 - place, place)


def lanes_of(shape):
    return lax.broadcasted_iota(jnp.int32, shape, 1)


def kernel(
    nt, nz, initial_hbm, guess_hbm, kappa_hbm, forcing_hbm, amp_hbm, out_ref,
    amp_ref, guess, pairs, windows, params, body, high, low, coarse, fine, amps, inner, inner_next, border, core, outer, outer_next, residual, error, edges, starts, packed, arrived,
    amp_sem, load_sem, pair_sem, win_send, win_recv, par_send, par_recv, z_send, z_recv, edge_send, edge_recv, back_send, back_recv,
):
    tm, z = lax.axis_index("tm"), lax.axis_index("space")
    tiles = guess.shape[1] // LANES
    widths = spans()
    has_up, has_down = z > 0, z < nz - 1
    mine = window_of(tm)
    before, after = window_of(lax.rem(mine + nt - 1, nt)), window_of(lax.rem(mine + 1, nt))

    barrier = pltpu.get_barrier_semaphore()

    def greet(t, where):
        pl.semaphore_signal(barrier, inc=1, device_id=(t, where), device_id_type=MESH)

    def greet_plane(k, carry):
        greet(lax.rem(tm + k, nt), z)
        return carry

    lax.fori_loop(1, nt, greet_plane, 0)

    @pl.when(has_up)
    def _():
        for t in (tm, before, after):
            greet(t, z - 1)

    @pl.when(has_down)
    def _():
        for t in (tm, before, after):
            greet(t, z + 1)

    load_guess = pltpu.make_async_copy(guess_hbm.at[0], guess, load_sem)
    load_guess.start()
    load_amps = pltpu.make_async_copy(amp_hbm, amp_ref, amp_sem)
    load_amps.start()
    first = lax.rem(lax.div(mine + nt - 1, 2), tiles)
    second = lax.rem(first + 1, tiles)
    loads = []
    for i, ref in enumerate((initial_hbm, kappa_hbm, forcing_hbm)):
        for k, tile in enumerate((first, second)):
            columns = pl.ds(pl.multiple_of(tile * LANES, LANES), LANES)
            loads.append(pltpu.make_async_copy(ref.at[:, columns], pairs.at[i, k], pair_sem.at[i, k]))
    for load in loads:
        load.start()

    def body_rows(t, first, count):
        return pl.ds(pl.multiple_of(t * ROWS + first, 8), count)

    def halo_rows(t, first, count):
        return pl.ds(pl.multiple_of(t * HALO + first, 8), count)

    def clear(ref, t, carry):
        ref[halo_rows(t, 0, HALO), :] = jnp.zeros((HALO, LANES), jnp.float32)
        return carry

    @pl.when(jnp.logical_not(has_up))
    def _():
        params[:, :HALO, :] = jnp.zeros((3, HALO, LANES), jnp.float32)
        lax.fori_loop(0, nt + 1, functools.partial(clear, high), 0)

    @pl.when(jnp.logical_not(has_down))
    def _():
        params[:, HALO + ROWS :, :] = jnp.zeros((3, HALO, LANES), jnp.float32)
        lax.fori_loop(0, nt + 1, functools.partial(clear, low), 0)

    @pl.when(jnp.logical_not(has_up))
    def _():
        edges[:, :, :SPAN, :] = jnp.zeros((nt // SPAN - 1, 3, SPAN, LANES), jnp.float32)

    @pl.when(jnp.logical_not(has_down))
    def _():
        edges[:, :, SPAN + ROWS :, :] = jnp.zeros((nt // SPAN - 1, 3, SPAN, LANES), jnp.float32)

    row_index = lax.broadcasted_iota(jnp.int32, (ROWS, LANES), 0)
    lane = lanes_of((ROWS, LANES))
    marks = jnp.zeros((ROWS, LANES), jnp.float32)
    load_amps.wait()
    for k in range(STEPS):
        marks = jnp.where(row_index == k, amp_ref[k], marks)
    marked = (lane == 0) & (row_index < STEPS)

    load_guess.wait()

    def tile_of(i):
        return guess[:, pl.ds(pl.multiple_of(i * LANES, LANES), LANES)]

    def cut(i, carry):
        low, mid, high = (tile_of(lax.rem(i + d, tiles)) for d in (tiles - 1, 0, 1))
        even = jnp.where(lane < SIDE, pltpu.roll(low, SIDE, 1), pltpu.roll(mid, SIDE, 1))
        odd = jnp.where(lane < LANES - SIDE, pltpu.roll(mid, LANES - SIDE, 1), pltpu.roll(high, LANES - SIDE, 1))
        windows[2 * i] = jnp.where(marked, marks, even)
        windows[2 * i + 1] = jnp.where(marked, marks, odd)
        return carry

    lax.fori_loop(0, tiles, cut, 0)
    pl.semaphore_wait(barrier, nt - 1 + 3 * has_up.astype(jnp.int32) + 3 * has_down.astype(jnp.int32))

    def window_copy(source, target):
        return pltpu.make_async_remote_copy(
            windows.at[window_of(target)], body.at[body_rows(source + 1, 0, ROWS)], win_send.at[target], win_recv.at[source],
            device_id=(target, z), device_id_type=MESH,
        )

    def send_window(k, carry):
        window_copy(tm, lax.rem(tm + k, nt)).start()
        return carry

    lax.fori_loop(1, nt, send_window, 0)
    body[body_rows(tm + 1, 0, ROWS), :] = windows[mine]

    for load in loads:
        load.wait()
    shift = jnp.where(lax.rem(mine, 2) == 0, SIDE, LANES - SIDE)
    for i in range(3):
        lower, upper = pltpu.roll(pairs[i, 0], shift, 1), pltpu.roll(pairs[i, 1], shift, 1)
        value = jnp.where(lane < shift, lower, upper)
        if i == 0:
            body[:ROWS, :] = value
        params[i, HALO : HALO + ROWS, :] = value

    def params_up():
        return pltpu.make_async_remote_copy(
            params.at[:, pl.ds(HALO, HALO)], params.at[:, pl.ds(HALO + ROWS, HALO)], par_send.at[0], par_recv.at[0],
            device_id=(tm, z - 1), device_id_type=MESH,
        )

    def params_down():
        return pltpu.make_async_remote_copy(
            params.at[:, pl.ds(ROWS, HALO)], params.at[:, pl.ds(0, HALO)], par_send.at[1], par_recv.at[1],
            device_id=(tm, z + 1), device_id_type=MESH,
        )

    def state_up(t, width):
        return pltpu.make_async_remote_copy(
            body.at[body_rows(t, 0, width)], low.at[halo_rows(t, 0, width)], z_send.at[0, t], z_recv.at[0, t],
            device_id=(tm, z - 1), device_id_type=MESH,
        )

    def state_down(t, width):
        return pltpu.make_async_remote_copy(
            body.at[body_rows(t, ROWS - width, width)], high.at[halo_rows(t, HALO - width, width)], z_send.at[1, t], z_recv.at[1, t],
            device_id=(tm, z + 1), device_id_type=MESH,
        )

    @pl.when(has_up)
    def _():
        params_up().start()

    @pl.when(has_down)
    def _():
        params_down().start()

    def forward(width, t, carry):
        @pl.when(t != tm + 1)
        def _():
            window_copy(t - 1, tm).wait_recv()

        @pl.when(has_up)
        def _():
            state_up(t, width).start()

        @pl.when(has_down)
        def _():
            state_down(t, width).start()

        return carry

    def forward_stage(s, carry):
        for first, last, width in widths:
            lax.fori_loop(jnp.maximum(s * SPAN + first, 1), s * SPAN + last, functools.partial(forward, width), 0)
        return carry

    lax.fori_loop(0, nt // SPAN, forward_stage, 0)

    @pl.when(tm != nt - 1)
    def _():
        window_copy(nt - 1, tm).wait_recv()

    def factors(i):
        rows = pl.ds(pl.multiple_of(i * GROUP, GROUP), GROUP)
        row = i * GROUP + lax.broadcasted_iota(jnp.int32, (GROUP, LANES), 0)
        inside = ((row >= HALO) | has_up) & ((row < HALO + ROWS) | has_down)
        kappa = params[1, rows, :]
        for ref, factor in ((fine, 1.0), (coarse, float(STEPS))):
            for k, value in enumerate((1.0 - factor * (4.0 * kappa + 2.0 * ADVECT), factor * (kappa + ADVECT), factor * kappa)):
                value = jnp.where(inside, value, 0.0)
                if ref is fine:
                    fine[k, rows] = jnp.broadcast_to(value[:, None, :], (GROUP, GROUP, LANES))
                else:
                    coarse[k, rows, :] = value
        forcing = jnp.where(inside, params[2, rows, :], 0.0)
        fine[3, rows] = jnp.broadcast_to(forcing[:, None, :], (GROUP, GROUP, LANES))

    def own_factors(i, carry):
        factors(HALO // GROUP + i)
        return carry

    lax.fori_loop(0, ROWS // GROUP, own_factors, 0)

    def body_at(t, r):
        return body[pl.ds(t * ROWS + r, GROUP, stride=ROWS), :]

    def halo_at(ref, t, r):
        return ref[pl.ds(t * HALO + r, GROUP, stride=HALO), :]

    def advance(load, store, amp, first, begin, end):
        for r in range(begin, end, BLOCK):
            n = min(BLOCK, end - r)
            u = load(r, n + 2)
            mid = u[1:-1]
            up_left = u[:-2] + pltpu.roll(mid, 1, 2)
            down_right = u[2:] + pltpu.roll(mid, LANES - 1, 2)
            centre, c_up, c_down, forcing = (fine[i, pl.ds(first + r, n)] for i in range(4))
            store(r, n, centre * mid + c_up * up_left + c_down * down_right + amp * forcing)

    def inner_step(source, target, s, k):
        for g in range(PAIR):
            border[s, g, k, 0:2] = source[g, pl.ds(k, 2)]
            border[s, g, k, 2:4] = source[g, pl.ds(ROWS - 2 - k, 2)]

            def load(r, n):
                return source[g, r : r + n]

            def store(r, n, value):
                target[g, r + 1 : r + 1 + n] = value

            advance(load, store, amps[s, g, k], HALO + 1, 0, ROWS - 2)

    def relax_inner(s, carry):
        for g in range(PAIR):
            t = s * SPAN + g * GROUP

            def load_amp(k, carry):
                amps[s, g, k] = jnp.broadcast_to(body_at(t + 1, k)[:, 0:1], (GROUP, LANES))
                return carry

            lax.fori_loop(0, STEPS, load_amp, 0, unroll=2)

            def load_rows(i, carry):
                for r in range(GROUP):
                    inner[g, i * GROUP + r] = body_at(t, i * GROUP + r)
                return carry

            lax.fori_loop(0, ROWS // GROUP, load_rows, 0)

        def two_steps(k, carry):
            inner_step(inner, inner_next, s, 2 * k)
            inner_step(inner_next, inner, s, 2 * k + 1)
            return carry

        lax.fori_loop(0, STEPS // 2, two_steps, 0)
        for g in range(PAIR):
            core[s, g] = inner[g, STEPS : STEPS + CORE]
        return carry

    lax.fori_loop(0, nt // SPAN, relax_inner, 0)

    @pl.when(has_down)
    def _():
        params_up().wait_recv()

    @pl.when(has_up)
    def _():
        params_down().wait_recv()

    high[:HALO, :] = params[0, :HALO, :]
    low[:HALO, :] = params[0, HALO + ROWS :, :]

    def halo_factors(i, carry):
        factors(jnp.where(i < HALO // GROUP, i, i + ROWS // GROUP))
        return carry

    lax.fori_loop(0, 2 * HALO // GROUP, halo_factors, 0)

    def arrive(width, t, carry):
        @pl.when(has_down)
        def _():
            state_up(t, width).wait_recv()

        @pl.when(has_up)
        def _():
            state_down(t, width).wait_recv()

        return carry

    def arrivals(s):
        for first, last, width in widths:
            lax.fori_loop(s * SPAN + max(first, 1), s * SPAN + last, functools.partial(arrive, width), 0)

        @pl.when(s < nt // SPAN - 1)
        def _():
            arrive(HALO, (s + 1) * SPAN, 0)

    def outer_step(source, target, s, k):
        for g in range(PAIR):
            for side in range(2):
                def load(r, n):
                    if side == 0 and r + n > HALO:
                        return jnp.concatenate([source[g, 0, r:HALO], border[s, g, k, 0 : r + n - HALO]], axis=0)
                    if side == 1 and r < 2:
                        return jnp.concatenate([border[s, g, k, 2 + r : 4], source[g, 1, 0 : r + n - 2]], axis=0)
                    first = r - 2 * side
                    return source[g, side, first : first + n]

                def store(r, n, value):
                    target[g, side, r : r + n] = value

                skip = g * GROUP
                if side == 0:
                    advance(load, store, amps[s, g, k], k + 1, skip, HALO)
                else:
                    advance(load, store, amps[s, g, k], HALO + ROWS - 1 - k, 0, HALO - skip)

    def relax(s):
        arrivals(s)
        for g in range(PAIR):
            t = s * SPAN + g * GROUP

            def load_rows(i, carry):
                for r in range(GROUP):
                    outer[g, 0, i * GROUP + r] = halo_at(high, t, i * GROUP + r)
                    outer[g, 1, i * GROUP + r] = halo_at(low, t, i * GROUP + r)
                return carry

            lax.fori_loop(0, HALO // GROUP, load_rows, 0)

        def two_steps(k, carry):
            outer_step(outer, outer_next, s, 2 * k)
            outer_step(outer_next, outer, s, 2 * k + 1)
            return carry

        lax.fori_loop(0, STEPS // 2, two_steps, 0)

        for g in range(PAIR):
            t = s * SPAN + g * GROUP

            def put(row, value):
                residual[s * PAIR + g, pl.ds(pl.multiple_of((row - STEPS) * GROUP, GROUP), GROUP), :] = value

            def finish_halo(i, carry):
                for r in range(GROUP):
                    row = i * GROUP + r
                    put(STEPS + row, outer[g, 0, row] - halo_at(high, t + 1, STEPS + row))
                    put(HALO + ROWS + row, outer[g, 1, STEPS + row] - halo_at(low, t + 1, row))
                return carry

            lax.fori_loop(0, (HALO - STEPS) // GROUP, finish_halo, 0)
            for r in range(STEPS):
                put(HALO + r, outer[g, 0, HALO - STEPS + r] - body_at(t + 1, r))
                put(HALO + ROWS - STEPS + r, outer[g, 1, r] - body_at(t + 1, ROWS - STEPS + r))

            def finish_core(i, carry):
                for r in range(GROUP):
                    row = i * GROUP + r
                    put(HALO + STEPS + row, core[s, g, row] - body_at(t + 1, STEPS + row))
                return carry

            lax.fori_loop(0, CORE // GROUP, finish_core, 0)

    def back_copy(source, target):
        return pltpu.make_async_remote_copy(
            packed.at[target], arrived.at[window_of(source)], back_send.at[target], back_recv.at[source],
            device_id=(target, z), device_id_type=MESH,
        )

    half = ROWS // 2
    lane_half = lanes_of((half, LANES))

    def sweep(group, e):
        centre, c_up, c_down = ([coarse[i, pl.ds(STEPS + b, 8, stride=8), :] for b in range(8)] for i in range(3))

        def step(place, e):
            t = group * GROUP + place
            above = [pltpu.roll(e[7], 1, 0)] + e[:7]
            below = e[1:] + [pltpu.roll(e[0], 7, 0)]
            after = []
            for b in range(8):
                up_left = above[b] + pltpu.roll(e[b], 1, 1)
                down_right = below[b] + pltpu.roll(e[b], LANES - 1, 1)
                add = residual[group, pl.ds(b * GROUP + place, 8, stride=8 * GROUP), :]
                after.append(centre[b] * e[b] + c_up[b] * up_left + c_down[b] * down_right + add)
            for b in range(8):
                error[t, pl.ds(b, 8, stride=8), :] = after[b]
            return after

        def pack(place):
            t = group * GROUP + place
            top, bottom = error[t, SPAN : SPAN + half, :], error[t, SPAN + half : SPAN + ROWS, :]
            packed[t] = jnp.where(lane_half < OWN, pltpu.roll(top, LANES - SIDE, 1), pltpu.roll(bottom, SIDE, 1))

        def pack_and_step(place, e):
            pack(place - 1)
            return step(place, e)

        e = lax.fori_loop(1, GROUP, pack_and_step, step(0, e), unroll=7)

        @pl.when((lax.rem(group, PAIR) == PAIR - 1) & (group < nt // GROUP - 1))
        def _():
            for dz, copy in edge_copies(lax.div(group, PAIR)):
                when_dz(dz, True, copy.start)

        pack(GROUP - 1)

        def give(t, carry):
            @pl.when(t != tm)
            def _():
                back_copy(tm, t).start()

            return carry

        lax.fori_loop(group * GROUP, (group + 1) * GROUP, give, 0)
        return e

    edge_rows = {-1: (pl.ds(SPAN, SPAN), pl.ds(SPAN + ROWS, SPAN)), 1: (pl.ds(ROWS, SPAN), pl.ds(0, SPAN)), 0: (pl.ds(SPAN, ROWS), pl.ds(SPAN, ROWS))}

    def edge_copies(s):
        for dz in (-1, 1, 0):
            for slot, target in ((2, before), (1, tm), (0, after)):
                if dz == 0 and slot == 1:
                    continue
                rows_here, rows_there = edge_rows[dz]
                copy = pltpu.make_async_remote_copy(
                    error.at[(s + 1) * SPAN - 1, rows_here], edges.at[s, slot, rows_there], edge_send.at[s, slot, dz + 1], edge_recv.at[s, slot, dz + 1],
                    device_id=(target, z + dz), device_id_type=MESH,
                )
                yield dz, copy

    def when_dz(dz, send, do):
        if dz == 0:
            do()
        else:
            up = (dz == -1) == send
            pl.when(has_up if up else has_down)(do)

    stages = nt // SPAN
    lane_trim = lanes_of((TRIM, LANES))
    row_trim = lax.broadcasted_iota(jnp.int32, (TRIM, LANES), 0)
    centre = (row_trim >= SPAN) & (row_trim < SPAN + ROWS)

    groups = SPAN // GROUP
    starts[...] = jnp.zeros((TRIM, LANES), jnp.float32)

    def stage(s, carry):
        relax(s)

        @pl.when(s > 0)
        def _():
            for dz, copy in edge_copies(s - 1):
                when_dz(dz, False, copy.wait_recv)
            left = pltpu.roll(edges[s - 1, 0], OWN, 1)
            right = pltpu.roll(edges[s - 1, 2], OWN, 1)
            own = jnp.where(centre, error[s * SPAN - 1], edges[s - 1, 1])
            starts[...] = jnp.where(lane_trim < SIDE, left, jnp.where(lane_trim >= LANES - SIDE, right, own))

        e = [starts[pl.ds(b, 8, stride=8), :] for b in range(8)]
        lax.fori_loop(s * groups, (s + 1) * groups, sweep, e)

        return carry

    lax.fori_loop(0, stages, stage, 0)

    def sent(k, carry):
        window_copy(tm, lax.rem(tm + k, nt)).wait_send()
        return carry

    lax.fori_loop(1, nt, sent, 0)

    def drain(copy):
        def drain_stage(s, carry):
            for first, last, width in widths:
                lax.fori_loop(
                    jnp.maximum(s * SPAN + first, 1), s * SPAN + last, lambda t, carry: (copy(t, width).wait_send(), carry)[1], 0
                )
            return carry

        lax.fori_loop(0, nt // SPAN, drain_stage, 0)

    @pl.when(has_up)
    def _():
        params_up().wait_send()
        drain(state_up)

    @pl.when(has_down)
    def _():
        params_down().wait_send()
        drain(state_down)

    for s in range(stages - 1):
        for dz, copy in edge_copies(s):
            when_dz(dz, True, copy.wait_send)

    def collect(k, carry):
        back_copy(lax.rem(tm + k, nt), tm).wait_recv()
        back_copy(tm, lax.rem(tm + k, nt)).wait_send()
        return carry

    lax.fori_loop(1, nt, collect, 0)

    def join(i, carry):
        first, second = arrived[2 * i], arrived[2 * i + 1]
        columns = pl.ds(pl.multiple_of(i * LANES, LANES), LANES)
        top = jnp.where(lane_half < OWN, first, pltpu.roll(second, OWN, 1))
        bottom = jnp.where(lane_half < OWN, pltpu.roll(first, OWN, 1), second)
        out_ref[0, :half, columns] = guess[:half, columns] + top
        out_ref[0, half:, columns] = guess[half:, columns] + bottom
        return carry

    arrived[mine] = packed[tm]
    lax.fori_loop(0, tiles, join, 0, unroll=8)


def per_device(initial_state, guesses, diffusivity, forcing_field, amplitudes):
    nt, nz = lax.axis_size("tm"), lax.axis_size("space")
    rows, cols = initial_state.shape
    stages = nt // SPAN
    dma = pltpu.SemaphoreType.DMA
    vmem = functools.partial(pltpu.VMEM, dtype=jnp.float32)
    hbm = pl.BlockSpec(memory_space=pl.ANY)
    return pl.pallas_call(
        functools.partial(kernel, nt, nz),
        out_shape=jax.ShapeDtypeStruct((1, rows, cols), jnp.float32),
        in_specs=[hbm] * 5,
        out_specs=pl.BlockSpec(memory_space=pltpu.VMEM),
        scratch_shapes=[
            pltpu.SMEM((STEPS,), jnp.float32),
            vmem((rows, cols)),
            vmem((3, 2, rows, LANES)),
            vmem((nt, rows, LANES)),
            vmem((3, TALL, LANES)),
            vmem(((nt + 1) * ROWS, LANES)),
            vmem(((nt + 1) * HALO, LANES)),
            vmem(((nt + 1) * HALO, LANES)),
            vmem((3, TALL, LANES)),
            vmem((4, TALL, GROUP, LANES)),
            vmem((nt // SPAN, PAIR, STEPS, GROUP, LANES)),
            vmem((PAIR, ROWS, GROUP, LANES)),
            vmem((PAIR, ROWS, GROUP, LANES)),
            vmem((nt // SPAN, PAIR, STEPS, 4, GROUP, LANES)),
            vmem((nt // SPAN, PAIR, CORE, GROUP, LANES)),
            vmem((PAIR, 2, HALO, GROUP, LANES)),
            vmem((PAIR, 2, HALO, GROUP, LANES)),
            vmem((nt // GROUP, TRIM * GROUP, LANES)),
            vmem((nt, TRIM, LANES)),
            vmem((stages - 1, 3, TRIM, LANES)),
            vmem((TRIM, LANES)),
            vmem((nt, rows // 2, LANES)),
            vmem((nt, rows // 2, LANES)),
            dma, dma, dma((3, 2)), dma((nt,)), dma((nt,)), dma((2,)), dma((2,)), dma((2, nt + 1)), dma((2, nt + 1)),
            dma((stages - 1, 3, 3)), dma((stages - 1, 3, 3)), dma((nt,)), dma((nt,)),
        ],
        compiler_params=pltpu.CompilerParams(collective_id=0, has_side_effects=True, vmem_limit_bytes=VMEM_LIMIT),
    )(initial_state, guesses, diffusivity, forcing_field, amplitudes)


def solution(mesh):
    placed = (P("space", None), P("tm", "space", None), P("space", None), P("space", None), P("tm"))
    return jax.shard_map(
        per_device, mesh=mesh, in_specs=placed, out_specs=P("tm", "space", None), check_vma=False
    )
```
